768 devices in a mesh: row: 24 (over y, z_lo), col: 32 (over x, z_hi, core).
Axes of the slice: x: 4, y: 8, z: 12 (z_hi: 4, z_lo: 3; z = z_hi * 3 + z_lo), core: 2. Of those that a mesh axis runs over, the one named last changes fastest.
Arguments:
- features: bfloat16 [98304, 512], P(('col', 'row')), may hold values from -6 to 6
- tile_values: bfloat16 [12288, 256, 256], P(('row', 'col')), as said below
- tile_rows: int32 [12288], P(('row', 'col')), may hold values from 0 to 15
- tile_cols: int32 [12288], P(('row', 'col')), may hold values from 0 to 11
- tile_live: int32 [768], P(('row', 'col')), may hold values from 4 to 16, as said below
- weight: bfloat16 [512, 512], replicated, may hold values from -0.25 to 0.25
- cotangent: bfloat16 [98304, 512], P(('row', 'col')), may hold values from -6 to 6
Outputs:
- hidden: bfloat16 [98304, 512], P(('row', 'col'))
- grad_features: bfloat16 [98304, 512], P(('col', 'row'))
- grad_weight: float32 [512, 512], replicated
The draws below stay inside these ranges and needn't reach their ends.
Inputs may be any that keep to these rules, and one draw needn't show every extreme that they name: `tile_live`: each block has 4 to 16 nonempty slots; some block has exactly 16 in every draw. `tile_values`: edge weights are non-negative.
All inputs are finite; a program needn't handle non-finite values.
Results may differ from the reference program's by a relative error of at most 0.02.
Values may be sent and summed in bfloat16 or wider, within the bound.
A program may use at most 128 MiB of HBM per device.

```python
import jax
import jax.numpy as jnp
from jax import lax

D = 512
TILE = 256
BLK_DEV = 128
SLOTS = 16
NODES = 98304
DEVS = 768
RT = 16
CT = 12
TILES = 12288
N_ROW = 24
N_COL = 32


def draw_tile_live(key, part):
    key = jax.random.fold_in(key, 11)
    key_counts, key_full = jax.random.split(key)
    counts = jax.random.randint(key_counts, (DEVS,), SLOTS // 4, SLOTS + 1)
    chosen = jax.random.randint(key_full, (), 0, DEVS)
    counts = jnp.where(jnp.arange(DEVS) == chosen, SLOTS, counts)
    return counts.astype(jnp.int32)


def draw_tile_values(key, part):
    key = jax.random.fold_in(key, 23)
    key_vals = jax.random.fold_in(key, 0)
    fan = float(SLOTS * TILE * TILE // BLK_DEV)
    top = (3.0 / fan) ** 0.5
    values = jax.random.uniform(key_vals, (TILES, TILE, TILE), jnp.float32, 0.0, top)
    return values.astype(jnp.bfloat16)


def set_ends(result, key, low, top_value):
    shape = result.shape
    spot = [jax.random.randint(jax.random.fold_in(key, axis), (), 0, shape[axis]) for axis in range(len(shape))]
    result = result.at[tuple(spot)].set(low)
    longest = shape.index(max(shape))
    spot[longest] = (spot[longest] + 1) % shape[longest]
    return result.at[tuple(spot)].set(top_value)


def block_levels(stream_key, dims, shards, least, largest):
    def one(position, blocks):
        steps = jax.random.uniform(jax.random.fold_in(jax.random.fold_in(stream_key, 6), position), (blocks,), jnp.float32, least / len(shards), largest / len(shards))
        return jnp.repeat(jnp.exp(steps), dims[position] // blocks).reshape((-1,) + (1,) * (len(dims) - position - 1))

    gain = one(*shards[0])
    for cut in shards[1:]:
        gain = gain * one(*cut)
    return gain


def bell_draw(own_key, shape, scale, limit, pieces=(), held_as=jnp.bfloat16):
    entries = jax.random.normal(own_key, shape, jnp.float32) * scale
    if len(pieces) > 0:
        entries = block_levels(own_key, shape, pieces, -0.22, 0.18) * entries
    return jnp.clip(entries, min=-limit, max=limit).astype(held_as)


def setup_inputs(seed: int = 0) -> dict:
    seeds = jax.random.split(jax.random.key(seed), 8)
    features = bell_draw(seeds[0], (NODES, D), 1.0, 6.0, ((0, 768),))
    tile_values = draw_tile_values(jax.random.fold_in(seeds[7], 71), 0)
    tile_rows = set_ends(jax.random.randint(seeds[2], (TILES,), 0, RT), jax.random.fold_in(seeds[2], 1), 0, RT - 1).astype(jnp.int32)
    tile_cols = set_ends(jax.random.randint(seeds[3], (TILES,), 0, CT), jax.random.fold_in(seeds[3], 1), 0, CT - 1).astype(jnp.int32)
    tile_live = draw_tile_live(jax.random.fold_in(seeds[7], 71), 0)
    weight = bell_draw(seeds[5], (D, D), D ** -0.5, 0.25)
    cotangent = bell_draw(seeds[6], (NODES, D), 1.0, 6.0, ((0, 768),))
    return {"features": features, "tile_values": tile_values, "tile_rows": tile_rows, "tile_cols": tile_cols, "tile_live": tile_live, "weight": weight, "cotangent": cotangent}


def reference(features, tile_values, tile_rows, tile_cols, tile_live, weight, cotangent):
    row_span = BLK_DEV * N_COL
    col_span = BLK_DEV * N_ROW
    tile_stack = tile_values.reshape(DEVS, SLOTS, TILE, TILE)
    slot_rows = tile_rows.reshape(DEVS, SLOTS)
    slot_cols = tile_cols.reshape(DEVS, SLOTS)
    slot_ids = jnp.arange(SLOTS, dtype=jnp.int32)

    def forward_step(running, device_index):
        block_row = (device_index // N_COL).astype(jnp.int32)
        block_col = (device_index % N_COL).astype(jnp.int32)
        source = lax.dynamic_slice_in_dim(features, block_col * col_span, col_span, 0)
        source = source.astype(jnp.float32).reshape(CT, TILE, D)
        picked = source[slot_cols[device_index]]
        live_mask = (slot_ids < tile_live[device_index]).astype(jnp.float32)
        products = jnp.einsum('kij,kjf->kif', tile_stack[device_index].astype(jnp.float32), picked,
                              precision=lax.Precision.HIGHEST) * live_mask[:, None, None]
        onehot = (slot_rows[device_index][:, None] == jnp.arange(RT, dtype=jnp.int32)[None, :]).astype(jnp.float32)
        partial_value = jnp.einsum('kr,kif->rif', onehot, products, precision=lax.Precision.HIGHEST).reshape(row_span, D)
        partial_value = lax.optimization_barrier(partial_value.astype(jnp.bfloat16)).astype(jnp.float32)
        current = lax.dynamic_slice_in_dim(running, block_row * row_span, row_span, 0)
        running = lax.dynamic_update_slice_in_dim(running, current + partial_value, block_row * row_span, 0)
        return running, None

    running, _ = lax.scan(forward_step, jnp.zeros((NODES, D), jnp.float32), jnp.arange(DEVS, dtype=jnp.int32))
    aggregated = running.astype(jnp.bfloat16)
    weight_f = weight.astype(jnp.float32)
    pre_act = jnp.dot(aggregated.astype(jnp.float32), weight_f, precision=lax.Precision.HIGHEST)
    sigmoid_z = jax.nn.sigmoid(pre_act)
    hidden = (pre_act * sigmoid_z).astype(jnp.bfloat16)
    grad_pre = (cotangent.astype(jnp.float32) * sigmoid_z * (1.0 + pre_act * (1.0 - sigmoid_z))).astype(jnp.bfloat16)
    grad_weight = jnp.dot(aggregated.astype(jnp.float32).T, grad_pre.astype(jnp.float32),
                          precision=lax.Precision.HIGHEST) * (float(NODES) ** -0.5)

    def backward_step(running, device_index):
        block_row = (device_index // N_COL).astype(jnp.int32)
        block_col = (device_index % N_COL).astype(jnp.int32)
        source = lax.dynamic_slice_in_dim(grad_pre, block_row * row_span, row_span, 0)
        source = source.astype(jnp.float32).reshape(RT, TILE, D)
        picked = source[slot_rows[device_index]]
        live_mask = (slot_ids < tile_live[device_index]).astype(jnp.float32)
        products = jnp.einsum('kji,kjf->kif', tile_stack[device_index].astype(jnp.float32), picked,
                              precision=lax.Precision.HIGHEST) * live_mask[:, None, None]
        onehot = (slot_cols[device_index][:, None] == jnp.arange(CT, dtype=jnp.int32)[None, :]).astype(jnp.float32)
        partial_value = jnp.einsum('kc,kif->cif', onehot, products, precision=lax.Precision.HIGHEST).reshape(col_span, D)
        partial_value = lax.optimization_barrier(partial_value.astype(jnp.bfloat16)).astype(jnp.float32)
        current = lax.dynamic_slice_in_dim(running, block_col * col_span, col_span, 0)
        running = lax.dynamic_update_slice_in_dim(running, current + partial_value, block_col * col_span, 0)
        return running, None

    back_sum, _ = lax.scan(backward_step, jnp.zeros((NODES, D), jnp.float32), jnp.arange(DEVS, dtype=jnp.int32))
    gathered_back = lax.optimization_barrier(back_sum.astype(jnp.bfloat16)).astype(jnp.float32)
    grad_features = jnp.dot(gathered_back, weight_f.T, precision=lax.Precision.HIGHEST).astype(jnp.bfloat16)
    return hidden, grad_features, grad_weight
```

```python
import functools

import jax
import jax.numpy as jnp
from jax import lax
from jax.experimental import pallas as pl
from jax.experimental.pallas import tpu as pltpu
from jax.sharding import PartitionSpec as P

MESH = pl.DeviceIdType.MESH
F32 = jnp.float32
BF16 = jnp.bfloat16
Z_LO = 3
Z_HI = 4
VMEM_LIMIT = 48 * 1024 * 1024
PART_A, CUT_A, CUT_B = 80, 48, 16


def wrap(value, size):
    return lax.rem(value + 2 * size, size)


def greet(peers):
    barrier = pltpu.get_barrier_semaphore()
    for peer in peers:
        pl.semaphore_signal(barrier, inc=1, device_id=peer, device_id_type=MESH)
    pl.semaphore_wait(barrier, len(peers))


class Links:
    def __init__(self, send, recv):
        self.send, self.recv, self.sent = send, recv, []

    def push(self, src, dst, peer, lands):
        i = len(self.sent)

        def copy(source, target):
            return pltpu.make_async_remote_copy(
                src_ref=source,
                dst_ref=target,
                send_sem=self.send.at[i],
                recv_sem=self.recv.at[i],
                device_id=peer,
                device_id_type=MESH,
            )

        out = copy(src, dst)
        out.start()
        self.sent.append(out)
        return copy(lands, lands).wait_recv

    def drain(self):
        for copy in self.sent:
            copy.wait_send()


def row_place(row):
    return lax.div(row, Z_LO), lax.rem(row, Z_LO)


def row_peers(y, z, rings):
    ups = [{"row": wrap(y + s, rings) * Z_LO + z} for s in (1, -1)]
    sides = [{"row": y * Z_LO + wrap(z + j, Z_LO)} for j in range(1, Z_LO)]
    return ups, sides


def gather_row_kernel(rings, feat_ref, out_ref, buf, send, recv, local):
    row = lax.axis_index("row")
    y, z = row_place(row)
    ups, sides = row_peers(y, z, rings)
    rows = feat_ref.shape[0]
    far = rings // 2
    parts = {"B": (PART_A, rows - PART_A, CUT_B)}
    for j in range(Z_LO):
        parts[j] = (0, PART_A, CUT_A)
    buf[row] = feat_ref[...]
    greet(ups + sides)
    links = Links(send, recv)

    def origin(y_off, z_off):
        return wrap(y + y_off, rings) * Z_LO + wrap(z + z_off, Z_LO)

    def span(tag, sign, hop):
        low, count, cut = parts[tag]
        if hop < far:
            return low, count
        return (low, cut) if sign > 0 else (low + cut, count - cut)

    def ring(tag, sign, hop):
        low, count = span(tag, sign, hop)
        z_off = 0 if tag == "B" else -tag
        mine = buf.at[origin(-sign * (hop - 1), z_off), pl.ds(low, count)]
        theirs = buf.at[origin(-sign * hop, z_off), pl.ds(low, count)]
        return links.push(mine, mine, ups[0 if sign > 0 else 1], theirs)

    def side(y_off, low, count):
        waits = []
        for j in range(1, Z_LO):
            mine = buf.at[origin(y_off, 0), pl.ds(low, count)]
            theirs = buf.at[origin(y_off, -j), pl.ds(low, count)]
            waits.append(links.push(mine, mine, sides[j - 1], theirs))
        return waits

    pending, last = {}, []

    def launch(tag):
        for sign in (1, -1):
            pending[tag, sign] = ring(tag, sign, 1)

    def step(tag, hop):
        for sign in (1, -1):
            pending[tag, sign]()
            if hop < far:
                pending[tag, sign] = ring(tag, sign, hop + 1)
            if tag == "B":
                last.extend(side(-sign * hop, *span(tag, sign, hop)))

    launch("B")
    launch(0)
    low, count, _ = parts[0]
    first = side(0, low, count)
    low, count, _ = parts["B"]
    last.extend(side(0, low, count))
    step("B", 1)
    step(0, 1)
    for j in range(1, Z_LO):
        first[j - 1]()
        launch(j)
    for hop in range(2, far + 1):
        step("B", hop)
        step(0, hop)
        for j in range(1, Z_LO):
            step(j, hop - 1)
    for j in range(1, Z_LO):
        step(j, far)
    for wait in last:
        wait()
    out = pltpu.make_async_copy(buf, out_ref, local)
    out.start()
    links.drain()
    out.wait()


def gather_row(features, n_row):
    rows, width = features.shape
    return pl.pallas_call(
        functools.partial(gather_row_kernel, n_row // Z_LO),
        out_shape=jax.ShapeDtypeStruct((n_row, rows, width), features.dtype),
        in_specs=[pl.BlockSpec(memory_space=pltpu.VMEM)],
        out_specs=pl.BlockSpec(memory_space=pl.ANY),
        scratch_shapes=[
            pltpu.VMEM((n_row, rows, width), features.dtype),
            pltpu.SemaphoreType.DMA((64,)),
            pltpu.SemaphoreType.DMA((64,)),
            pltpu.SemaphoreType.DMA,
        ],
        compiler_params=pltpu.CompilerParams(
            collective_id=0, has_side_effects=True, vmem_limit_bytes=VMEM_LIMIT
        ),
        name="gather_row",
    )(features)


def tiles_kernel(transposed, live, into, origin, tiles, source, out, total):
    total[...] = jnp.zeros_like(total)

    def slot(k, _):
        at = into[k]
        total[at] += lax.dot_general(
            tiles[k],
            source[origin[k]],
            (((0 if transposed else 1,), (0,)), ((), ())),
            preferred_element_type=F32,
        )
        return 0

    lax.fori_loop(0, live[0], slot, 0)
    out[...] = total[...].astype(out.dtype)


def tile_products(tiles, source, live, into, origin, count, transposed):
    edge, width = source.shape[1:]
    smem = pl.BlockSpec(memory_space=pltpu.SMEM)
    vmem = pl.BlockSpec(memory_space=pltpu.VMEM)
    return pl.pallas_call(
        functools.partial(tiles_kernel, transposed),
        out_shape=jax.ShapeDtypeStruct((count, edge, width), BF16),
        in_specs=[smem, smem, smem, vmem, vmem],
        out_specs=vmem,
        scratch_shapes=[pltpu.VMEM((count, edge, width), F32)],
        compiler_params=pltpu.CompilerParams(vmem_limit_bytes=VMEM_LIMIT),
        name="tiles_back" if transposed else "tiles_forward",
    )(live, into, origin, tiles, source)


def layer_kernel(
    n_x,
    part_ref,
    weight_ref,
    cot_ref,
    hidden_ref,
    grads_ref,
    local_ref,
    sums,
    from_core,
    x_far,
    x_near,
    z_sums,
    z_far,
    z_near,
    grads,
    send,
    recv,
    local,
):
    col = lax.axis_index("col")
    core = lax.rem(col, 2)
    chip = lax.div(col, 2)
    x, z = lax.div(chip, Z_HI), lax.rem(chip, Z_HI)
    rows = part_ref.shape[1]
    half = rows // 2

    def place(x_off, z_off, k):
        return (wrap(x + x_off, n_x) * Z_HI + wrap(z + z_off, Z_HI)) * 2 + k

    sibling = {"col": place(0, 0, 1 - core)}
    along_x = {s: {"col": place(s, 0, core)} for s in (1, -1)}
    along_z = {s: {"col": place(0, s, core)} for s in (1, -1)}
    greet([sibling, along_x[1], along_x[-1], along_z[1], along_z[-1]])
    links = Links(send, recv)
    order = (2, 1, -1, 0)
    full = pl.ds(0, rows)
    piece = {1: pl.ds(0, half), -1: pl.ds(half, half)}

    arrived = {}
    for g, z_off in enumerate(order):
        for i, x_off in enumerate(order):
            slot = from_core.at[g, i]
            arrived[g, i] = links.push(part_ref.at[place(x_off, z_off, 1 - core)], slot, sibling, slot)

    def pair_sum(g, i):
        arrived[g, i]()
        mine = part_ref[place(order[i], order[g], core)].astype(F32)
        sums[g, i] = (mine + from_core[g, i].astype(F32)).astype(BF16)

    def add(target, at, other):
        target[at] = (target[at].astype(F32) + other.astype(F32)).astype(BF16)

    waits = {}

    def x_first(g):
        pair_sum(g, 0)
        for n, s in enumerate((1, -1)):
            slot = x_far.at[g, n]
            waits[g, "far", s] = links.push(sums.at[g, 0, piece[s]], slot, along_x[s], slot)

    def x_second(g):
        for n, s in enumerate((1, -1)):
            pair_sum(g, 1 + n)
            waits[g, "far", s]()
            add(sums, (g, 1 + n, piece[s]), x_far[g, n])
            slot = x_near.at[g, n]
            waits[g, "near", s] = links.push(sums.at[g, 1 + n], slot, along_x[s], slot)

    def x_last(g):
        pair_sum(g, 3)
        for s in (1, -1):
            waits[g, "near", s]()
        total = sums[g, 3].astype(F32) + x_near[g, 0].astype(F32) + x_near[g, 1].astype(F32)
        z_sums[g] = total.astype(BF16)

    z_waits = {}

    def z_first():
        for n, s in enumerate((1, -1)):
            slot = z_far.at[n]
            z_waits["far", s] = links.push(z_sums.at[0, piece[s]], slot, along_z[s], slot)

    def z_second(g):
        n, s = g - 1, order[g]
        z_waits["far", s]()
        add(z_sums, (g, piece[s]), z_far[n])
        slot = z_near.at[n]
        z_waits["near", s] = links.push(z_sums.at[g], slot, along_z[s], slot)

    x_first(0)
    x_first(1)
    x_second(0)
    x_first(2)
    x_second(1)
    x_last(0)
    z_first()
    x_first(3)
    x_second(2)
    x_last(1)
    z_second(1)
    x_second(3)
    x_last(2)
    z_second(2)
    x_last(3)
    for s in (1, -1):
        z_waits["near", s]()
    total = z_sums[3].astype(F32) + z_near[0].astype(F32) + z_near[1].astype(F32)
    own_sum = total.astype(BF16)

    pre_act = jnp.dot(own_sum, weight_ref[...], preferred_element_type=F32)
    gate = jax.nn.sigmoid(pre_act)
    own_grad = (cot_ref[...].astype(F32) * gate * (1.0 + pre_act * (1.0 - gate))).astype(BF16)
    grads[col] = own_grad

    last = []

    def chunk(x_off, z_off, k, where):
        return grads.at[place(x_off, z_off, k), where]

    def to_core(x_off, z_off, where):
        mine = chunk(x_off, z_off, core, where)
        last.append(links.push(mine, mine, sibling, chunk(x_off, z_off, 1 - core, where)))

    def to_z(s, z_off, where):
        mine = chunk(0, z_off, core, where)
        return links.push(mine, mine, along_z[s], chunk(0, z_off - s, core, where))

    def to_x(s, x_off, z_off, where):
        mine = chunk(x_off, z_off, core, where)
        return links.push(mine, mine, along_x[s], chunk(x_off - s, z_off, core, where))

    def cut(where):
        size = where.size // 2
        return {1: pl.ds(where.start, size), -1: pl.ds(where.start + size, size)}

    def x_start(z_off, where):
        return {s: to_x(s, 0, z_off, where) for s in (1, -1)}

    def x_pass(near, z_off, where):
        far = {}
        for s in (1, -1):
            near[s]()
            far[s] = to_x(s, -s, z_off, cut(where)[s])
            to_core(-s, z_off, where)
        return far

    def x_end(far, z_off, where):
        for s in (1, -1):
            far[s]()
            to_core(2, z_off, cut(where)[s])

    near_z = {s: to_z(s, 0, full) for s in (1, -1)}
    near = [x_start(0, full)]
    to_core(0, 0, full)
    hidden_ref[...] = (pre_act * gate).astype(hidden_ref.dtype)
    local_ref[...] = lax.dot_general(
        own_sum, own_grad, (((0,), (0,)), ((), ())), preferred_element_type=F32
    )
    far_z = {}
    for s in (1, -1):
        near_z[s]()
        far_z[s] = to_z(s, -s, piece[s])
        near.append(x_start(-s, full))
        to_core(0, -s, full)
    far = [x_pass(near[0], 0, full)]
    for s in (1, -1):
        far_z[s]()
        near.append(x_start(2, piece[s]))
        to_core(0, 2, piece[s])
    spans = [(0, full), (-1, full), (1, full), (2, piece[1]), (2, piece[-1])]
    for i in range(1, 5):
        far.append(x_pass(near[i], *spans[i]))
        x_end(far[i - 1], *spans[i - 1])
    x_end(far[4], *spans[4])
    for wait in last:
        wait()
    out = pltpu.make_async_copy(grads, grads_ref, local)
    out.start()
    links.drain()
    out.wait()


def layer(partial, weight, cotangent, n_col):
    _, rows, width = partial.shape
    vmem = pl.BlockSpec(memory_space=pltpu.VMEM)
    return pl.pallas_call(
        functools.partial(layer_kernel, n_col // (2 * Z_HI)),
        out_shape=(
            jax.ShapeDtypeStruct((rows, width), BF16),
            jax.ShapeDtypeStruct((n_col, rows, width), BF16),
            jax.ShapeDtypeStruct((width, width), F32),
        ),
        in_specs=[vmem, vmem, vmem],
        out_specs=(vmem, pl.BlockSpec(memory_space=pl.ANY), vmem),
        scratch_shapes=[
            pltpu.VMEM((4, 4, rows, width), BF16),
            pltpu.VMEM((4, 4, rows, width), BF16),
            pltpu.VMEM((4, 2, rows // 2, width), BF16),
            pltpu.VMEM((4, 2, rows, width), BF16),
            pltpu.VMEM((4, rows, width), BF16),
            pltpu.VMEM((2, rows // 2, width), BF16),
            pltpu.VMEM((2, rows, width), BF16),
            pltpu.VMEM((n_col, rows, width), BF16),
            pltpu.SemaphoreType.DMA((96,)),
            pltpu.SemaphoreType.DMA((96,)),
            pltpu.SemaphoreType.DMA,
        ],
        compiler_params=pltpu.CompilerParams(
            collective_id=1, has_side_effects=True, vmem_limit_bytes=VMEM_LIMIT
        ),
        name="layer",
    )(partial, weight, cotangent)


def finish_kernel(
    rings,
    n_x,
    scale,
    part_ref,
    weight_ref,
    local_ref,
    out_ref,
    gw_ref,
    a_in,
    a_sum,
    a_side,
    b_in,
    b_sum,
    b_side,
    w_core,
    w_x,
    w_y,
    w_lo,
    w_hi,
    w_piece,
    w_sum,
    send,
    recv,
):
    row, col = lax.axis_index("row"), lax.axis_index("col")
    y, z = row_place(row)
    core = lax.rem(col, 2)
    chip = lax.div(col, 2)
    x, z_hi = lax.div(chip, Z_HI), lax.rem(chip, Z_HI)
    rows = part_ref.shape[1]
    far = rings // 2
    ups, sides = row_peers(y, z, rings)
    up = {1: ups[0], -1: ups[1]}
    sibling = {"col": chip * 2 + 1 - core}
    x_peers = [{"col": (wrap(x + j, n_x) * Z_HI + z_hi) * 2 + core} for j in range(1, n_x)]
    y_peers = [{"row": wrap(y + j, rings) * Z_LO + z} for j in range(1, rings)]
    hi_peers = [{"col": (x * Z_HI + wrap(z_hi + j, Z_HI)) * 2 + core} for j in range(1, Z_HI)]
    greet([sibling] + x_peers + y_peers + sides + hi_peers)
    links = Links(send, recv)

    def dest(y_off, z_off):
        return wrap(y + y_off, rings) * Z_LO + wrap(z + z_off, Z_LO)

    depth = local_ref.shape[0]
    n_pair, n_quarter, n_piece = depth // 2, depth // 2 // n_x, depth // 2 // n_x // rings

    def stage_core():
        return [
            links.push(local_ref.at[pl.ds((1 - core) * n_pair, n_pair)], w_core, sibling, w_core)
        ]

    def stage_x():
        w_sum[...] = local_ref[pl.ds(core * n_pair, n_pair)] + w_core[...]
        return [
            links.push(w_sum.at[pl.ds(wrap(x + j, n_x) * n_quarter, n_quarter)], w_x.at[j - 1], x_peers[j - 1], w_x.at[j - 1])
            for j in range(1, n_x)
        ]

    def stage_y():
        mine = pl.ds(x * n_quarter, n_quarter)
        total = w_sum[mine]
        for j in range(1, n_x):
            total += w_x[j - 1]
        w_sum[mine] = total
        return [
            links.push(
                w_sum.at[pl.ds(x * n_quarter + wrap(y + j, rings) * n_piece, n_piece)],
                w_y.at[j - 1],
                y_peers[j - 1],
                w_y.at[j - 1],
            )
            for j in range(1, rings)
        ]

    def stage_lo():
        total = w_sum[pl.ds(x * n_quarter + y * n_piece, n_piece)]
        for j in range(1, rings):
            total += w_y[j - 1]
        w_piece[0] = total
        return [links.push(w_piece.at[0], w_lo.at[j - 1], sides[j - 1], w_lo.at[j - 1]) for j in range(1, Z_LO)]

    def stage_hi():
        total = w_piece[0]
        for j in range(1, Z_LO):
            total += w_lo[j - 1]
        w_piece[1] = total
        return [links.push(w_piece.at[1], w_hi.at[j - 1], hi_peers[j - 1], w_hi.at[j - 1]) for j in range(1, Z_HI)]

    def back(y_off, x_off, k, count):
        base = k * n_pair + wrap(x + x_off, n_x) * n_quarter + wrap(y + y_off, rings) * n_piece
        return gw_ref.at[pl.ds(base, count)]

    def stage_back_y():
        total = w_piece[1]
        for j in range(1, Z_HI):
            total += w_hi[j - 1]
        gw_ref[pl.ds(core * n_pair + x * n_quarter + y * n_piece, n_piece)] = total * scale
        mine = back(0, 0, core, n_piece)
        return [links.push(mine, mine, y_peers[j - 1], back(-j, 0, core, n_piece)) for j in range(1, rings)]

    def quarter(x_off, k):
        return gw_ref.at[pl.ds(k * n_pair + wrap(x + x_off, n_x) * n_quarter, n_quarter)]

    def stage_back_x():
        mine = quarter(0, core)
        return [links.push(mine, mine, x_peers[j - 1], quarter(-j, core)) for j in range(1, n_x)]

    def stage_back_core():
        mine = gw_ref.at[pl.ds(core * n_pair, n_pair)]
        return [links.push(mine, mine, sibling, gw_ref.at[pl.ds((1 - core) * n_pair, n_pair)])]

    stages = [stage_core, stage_x, stage_y, stage_lo, stage_hi, stage_back_y, stage_back_x, stage_back_core]
    weight_waits = []

    def weight_step():
        for wait in weight_waits:
            wait()
        del weight_waits[:]
        if stages:
            weight_waits.extend(stages.pop(0)())

    waits = {}

    def half(low, count, cut, sign):
        return pl.ds(low, cut) if sign > 0 else pl.ds(low + cut, count - cut)

    def a_send(j, hop):
        for n, s in enumerate((1, -1)):
            at = a_sum.at[j, n, hop - 1]
            slot = a_in.at[j, n, hop - 1]
            if hop == far:
                where = half(0, PART_A, CUT_A, s)
                a_sum[j, n, hop - 1, where] = part_ref[dest(s * hop, j), where]
                at, slot = at.at[where], slot.at[where]
            else:
                mine = part_ref[dest(s * hop, j), pl.ds(0, PART_A)]
                waits["A", j, s]()
                if hop + 1 == far:
                    a_sum[j, n, hop - 1] = mine
                    where = half(0, PART_A, CUT_A, s)
                    both = a_sum[j, n, hop - 1, where].astype(F32) + a_in[j, n, hop, where].astype(F32)
                    a_sum[j, n, hop - 1, where] = both.astype(BF16)
                else:
                    a_sum[j, n, hop - 1] = (mine.astype(F32) + a_in[j, n, hop].astype(F32)).astype(BF16)
            waits["A", j, s] = links.push(at, slot, up[s], slot)

    def a_total(j):
        for s in (1, -1):
            waits["A", j, s]()
        mine = part_ref[dest(0, j), pl.ds(0, PART_A)].astype(F32)
        return mine + a_in[j, 0, 0].astype(F32) + a_in[j, 1, 0].astype(F32)

    side_waits = []

    def a_across(j):
        a_side[0, j - 1] = a_total(j).astype(BF16)
        slot = a_side.at[1, j - 1]
        side_waits.append(links.push(a_side.at[0, j - 1], slot, sides[j - 1], slot))

    n_b = rows - PART_A
    part_b = pl.ds(PART_A, n_b)
    offsets = [far] + [s * h for h in range(far - 1, 0, -1) for s in (1, -1)] + [0]
    b_waits = {}

    def b_across():
        for i, y_off in enumerate(offsets):
            b_waits[y_off] = []
            for j in range(1, Z_LO):
                slot = b_side.at[i, j - 1]
                b_waits[y_off].append(
                    links.push(part_ref.at[dest(y_off, j), part_b], slot, sides[j - 1], slot)
                )

    def b_total(y_off):
        i = offsets.index(y_off)
        for wait in b_waits[y_off]:
            wait()
        mine = part_ref[dest(y_off, 0), part_b].astype(F32)
        return mine + b_side[i, 0].astype(F32) + b_side[i, 1].astype(F32)

    def b_send(hop):
        if hop == far:
            b_sum[0, far - 1] = b_total(far).astype(BF16)
        for n, s in enumerate((1, -1)):
            if hop == far:
                where = half(0, n_b, CUT_B, s)
                at, slot = b_sum.at[0, hop - 1, where], b_in.at[n, hop - 1, where]
            else:
                total = b_total(s * hop)
                at, slot = b_sum.at[n, hop - 1], b_in.at[n, hop - 1]
                waits["B", s]()
                if hop + 1 == far:
                    where = half(0, n_b, CUT_B, s)
                    b_sum[n, hop - 1] = total.astype(BF16)
                    both = b_sum[n, hop - 1, where].astype(F32) + b_in[n, hop, where].astype(F32)
                    b_sum[n, hop - 1, where] = both.astype(BF16)
                else:
                    b_sum[n, hop - 1] = (total + b_in[n, hop].astype(F32)).astype(BF16)
            waits["B", s] = links.push(at, slot, up[s], slot)

    for j in (1, 2, 0):
        a_send(j, far)
    b_across()
    weight_step()
    for hop in range(far - 1, 0, -1):
        for j in (1, 2):
            a_send(j, hop)
        weight_step()
        b_send(hop + 1)
        a_send(0, hop)
        weight_step()
    for j in (1, 2):
        a_across(j)
    b_send(1)
    weight_step()
    total_a = a_total(0)
    total_b = b_total(0)
    for s in (1, -1):
        waits["B", s]()
    total_b += b_in[0, 0].astype(F32) + b_in[1, 0].astype(F32)
    for j, wait in enumerate(side_waits):
        wait()
        total_a += a_side[1, j].astype(F32)
    for where, total in ((pl.ds(0, PART_A), total_a), (part_b, total_b)):
        out_ref[where] = lax.dot_general(
            total.astype(BF16), weight_ref[...], (((1,), (1,)), ((), ())), preferred_element_type=F32
        ).astype(out_ref.dtype)
    while stages or weight_waits:
        weight_step()
    links.drain()


def finish(partial, weight, local, n_row, n_col, scale):
    _, rows, width = partial.shape
    rings, n_x = n_row // Z_LO, n_col // (2 * Z_HI)
    far, n_b = rings // 2, rows - PART_A
    depth = width // 2
    vmem = pl.BlockSpec(memory_space=pltpu.VMEM)
    return pl.pallas_call(
        functools.partial(finish_kernel, rings, n_x, scale),
        out_shape=(
            jax.ShapeDtypeStruct((rows, width), BF16),
            jax.ShapeDtypeStruct((width, width), F32),
        ),
        in_specs=[vmem, vmem, vmem],
        out_specs=(vmem, vmem),
        scratch_shapes=[
            pltpu.VMEM((Z_LO, 2, far, PART_A, width), BF16),
            pltpu.VMEM((Z_LO, 2, far, PART_A, width), BF16),
            pltpu.VMEM((2, Z_LO - 1, PART_A, width), BF16),
            pltpu.VMEM((2, far, n_b, width), BF16),
            pltpu.VMEM((2, far, n_b, width), BF16),
            pltpu.VMEM((rings, Z_LO - 1, n_b, width), BF16),
            pltpu.VMEM((depth, width), F32),
            pltpu.VMEM((n_x - 1, depth // n_x, width), F32),
            pltpu.VMEM((rings - 1, depth // n_x // rings, width), F32),
            pltpu.VMEM((Z_LO - 1, depth // n_x // rings, width), F32),
            pltpu.VMEM((Z_HI - 1, depth // n_x // rings, width), F32),
            pltpu.VMEM((2, depth // n_x // rings, width), F32),
            pltpu.VMEM((depth, width), F32),
            pltpu.SemaphoreType.DMA((128,)),
            pltpu.SemaphoreType.DMA((128,)),
        ],
        compiler_params=pltpu.CompilerParams(
            collective_id=2, has_side_effects=True, vmem_limit_bytes=VMEM_LIMIT
        ),
        name="finish",
    )(partial, weight, local)


def shards(features, tile_values, tile_rows, tile_cols, tile_live, weight, cotangent):
    rows, width = features.shape
    edge = tile_values.shape[1]
    n_row, n_col = lax.axis_size("row"), lax.axis_size("col")
    row_tiles, col_tiles = rows * n_col // edge, rows * n_row // edge
    column_block = gather_row(features, n_row).reshape(col_tiles, edge, width)
    partial = tile_products(
        tile_values, column_block, tile_live, tile_rows, tile_cols, row_tiles, False
    )
    hidden, grads, local = layer(partial.reshape(n_col, rows, width), weight, cotangent, n_col)
    back = tile_products(
        tile_values,
        grads.reshape(row_tiles, edge, width),
        tile_live,
        tile_cols,
        tile_rows,
        col_tiles,
        True,
    )
    scale = float(rows * n_row * n_col) ** -0.5
    grad_features, grad_weight = finish(
        back.reshape(n_row, rows, width), weight, local, n_row, n_col, scale
    )
    return hidden, grad_features, grad_weight


def solution(mesh):
    return jax.shard_map(
        shards,
        mesh=mesh,
        in_specs=(
            P(("col", "row"), None),
            P(("row", "col"), None, None),
            P(("row", "col")),
            P(("row", "col")),
            P(("row", "col")),
            P(),
            P(("row", "col"), None),
        ),
        out_specs=(P(("row", "col"), None), P(("col", "row"), None), P()),
        check_vma=False,
    )
```

```python
import functools

import jax
import jax.numpy as jnp
from jax import lax
from jax.experimental import pallas as pl
from jax.experimental.pallas import tpu as pltpu
from jax.sharding import PartitionSpec as P

MESH = pl.DeviceIdType.MESH
F32 = jnp.float32
BF16 = jnp.bfloat16
Z_LO = 3
Z_HI = 4
VMEM_LIMIT = 58 * 1024 * 1024
GATHER_PART, GATHER_CUTS = 64, (32, 32)
SUM_PART, SUM_CUTS = 80, (48, 16)


def wrap(value, size):
    return lax.rem(value + 2 * size, size)


class Links:
    def __init__(self, send, recv):
        self.send, self.recv, self.count, self.sent = send, recv, 0, []

    def push(self, src, dst, peer, lands):
        i = self.count
        self.count += 1

        def copy(source, target):
            return pltpu.make_async_remote_copy(
                src_ref=source,
                dst_ref=target,
                send_sem=self.send.at[i],
                recv_sem=self.recv.at[i],
                device_id=peer,
                device_id_type=MESH,
            )

        out = copy(src, dst)
        out.start()
        self.sent.append(out)
        return copy(lands, lands).wait_recv

    def drain(self):
        for copy in self.sent:
            copy.wait_send()
        self.sent = []


class Place:
    def __init__(self, rings, n_x):
        self.rings, self.n_x = rings, n_x
        self.row, self.col = lax.axis_index("row"), lax.axis_index("col")
        self.y, self.zl = lax.div(self.row, Z_LO), lax.rem(self.row, Z_LO)
        self.chip, self.core = lax.div(self.col, 2), lax.rem(self.col, 2)
        self.x, self.zh = lax.div(self.chip, Z_HI), lax.rem(self.chip, Z_HI)
        self.sibling = {"col": self.chip * 2 + 1 - self.core}
        self.xs = {j: {"col": self.chip_at(j, 0) * 2 + self.core} for j in range(1, n_x)}
        self.zhs = {j: {"col": self.chip_at(0, j) * 2 + self.core} for j in range(1, Z_HI)}
        self.ys = {j: {"row": self.row_at(j, 0)} for j in range(1, rings)}
        self.zls = {j: {"row": self.row_at(0, j)} for j in range(1, Z_LO)}
        for peers, size in ((self.xs, n_x), (self.zhs, Z_HI), (self.ys, rings), (self.zls, Z_LO)):
            peers[-1] = peers[size - 1]

    def chip_at(self, x_off, z_off):
        return wrap(self.x + x_off, self.n_x) * Z_HI + wrap(self.zh + z_off, Z_HI)

    def row_at(self, y_off, z_off):
        return wrap(self.y + y_off, self.rings) * Z_LO + wrap(self.zl + z_off, Z_LO)

    def greet(self):
        barrier = pltpu.get_barrier_semaphore()
        peers = [self.sibling]
        for group in (self.xs, self.zhs, self.ys, self.zls):
            peers += [peer for j, peer in group.items() if j > 0]
        for peer in peers:
            pl.semaphore_signal(barrier, inc=1, device_id=peer, device_id_type=MESH)
        pl.semaphore_wait(barrier, len(peers))


def chunk(ref, index, rows=None):
    at = ref.at[lax.div(index, 2), lax.rem(index, 2)]
    return at if rows is None else at.at[rows]


def gather_row(here, links, buf):
    rows = buf.shape[2]
    far = here.rings // 2
    parts = {"B": (GATHER_PART, rows - GATHER_PART, GATHER_CUTS[1])}
    for j in range(Z_LO):
        parts[j] = (0, GATHER_PART, GATHER_CUTS[0])

    def span(tag, sign, hop):
        low, count, cut = parts[tag]
        if hop < far:
            return pl.ds(low, count)
        return pl.ds(low, cut) if sign > 0 else pl.ds(low + cut, count - cut)

    def ring(tag, sign, hop):
        where = span(tag, sign, hop)
        z_off = 0 if tag == "B" else -tag
        mine = chunk(buf, here.row_at(-sign * (hop - 1), z_off), where)
        theirs = chunk(buf, here.row_at(-sign * hop, z_off), where)
        return links.push(mine, mine, here.ys[sign], theirs)

    def side(y_off, where):
        waits = []
        for j in range(1, Z_LO):
            mine = chunk(buf, here.row_at(y_off, 0), where)
            theirs = chunk(buf, here.row_at(y_off, -j), where)
            waits.append(links.push(mine, mine, here.zls[j], theirs))
        return waits

    pending, last = {}, []

    def launch(tag):
        for sign in (1, -1):
            pending[tag, sign] = ring(tag, sign, 1)

    def step(tag, hop):
        for sign in (1, -1):
            pending[tag, sign]()
            if hop < far:
                pending[tag, sign] = ring(tag, sign, hop + 1)
            if tag == "B":
                last.extend(side(-sign * hop, span(tag, sign, hop)))

    launch("B")
    launch(0)
    first = side(0, span(0, 1, 1))
    last.extend(side(0, span("B", 1, 1)))
    step("B", 1)
    step(0, 1)
    for j in range(1, Z_LO):
        first[j - 1]()
        launch(j)
    for hop in range(2, far + 1):
        step("B", hop)
        step(0, hop)
        for j in range(1, Z_LO):
            step(j, hop - 1)
    for j in range(1, Z_LO):
        step(j, far)
    for wait in last:
        wait()


def tile_products(tiles, source, into, origin, total, transposed):
    slots = tiles.shape[0]
    total[slots] = jnp.zeros(total.shape[1:], F32)

    def slot(k, _):
        before = jnp.int32(slots)
        for j in range(slots):
            before = jnp.where((j < k) & (into[j] == into[k]), j, before)
        block = source[origin[k]]
        total[k] = total[before] + lax.dot_general(
            tiles[k],
            block.reshape(block.shape[0] * block.shape[1], block.shape[2]),
            (((0 if transposed else 1,), (0,)), ((), ())),
            preferred_element_type=F32,
        )
        return 0

    lax.fori_loop(0, slots, slot, 0)


def target_sum(total, into, live, target):
    slots = total.shape[0] - 1
    count = live[0]
    last = jnp.int32(slots)
    for j in range(slots):
        last = jnp.where((j < count) & (into[j] == target), j, last)
    return total[last]


ORDER = (2, 1, -1, 0)


def sum_col(here, links, tile, part, from_core, sums, x_far, x_near, z_sums, z_far, z_near):
    rows, width = part.shape[2:]
    half, quarter = rows // 2, rows // 4
    halves = (pl.ds(0, half), pl.ds(half, half))
    core = here.core
    arrived = {}
    for g, z_off in enumerate(ORDER):
        for i, x_off in enumerate(ORDER):
            chip = here.chip_at(x_off, z_off)
            part[chip] = tile(chip).astype(BF16).reshape(2, rows, width)
            slot = from_core.at[g, i]
            arrived[g, i] = links.push(part.at[chip, 1 - core], slot, here.sibling, slot)

    def pair_sum(g, i):
        if (g, i) in arrived:
            arrived.pop((g, i))()
            sums[g, i] = part[here.chip_at(ORDER[i], ORDER[g]), core] + from_core[g, i]

    def quarter_of(h, s):
        return pl.ds(h * half + (0 if s > 0 else quarter), quarter)

    waits = {}

    def x_first(b):
        g, h = b
        pair_sum(g, 0)
        for n, s in enumerate((1, -1)):
            slot = x_far.at[g, h, n]
            waits[b, "far", s] = links.push(sums.at[g, 0, quarter_of(h, s)], slot, here.xs[s], slot)

    def x_second(b):
        g, h = b
        for n, s in enumerate((1, -1)):
            pair_sum(g, 1 + n)
            waits[b, "far", s]()
            where = quarter_of(h, s)
            sums[g, 1 + n, where] = sums[g, 1 + n, where] + x_far[g, h, n]
            slot = x_near.at[g, h, n]
            waits[b, "near", s] = links.push(sums.at[g, 1 + n, halves[h]], slot, here.xs[s], slot)

    def x_last(b):
        g, h = b
        pair_sum(g, 3)
        for s in (1, -1):
            waits[b, "near", s]()
        total = sums[g, 3, halves[h]].astype(F32) + x_near[g, h, 0].astype(F32) + x_near[g, h, 1].astype(F32)
        z_sums[g, halves[h]] = total.astype(BF16)
        if g == 0:
            n, s = h, (1, -1)[h]
            slot = z_far.at[n]
            waits["z_far", s] = links.push(z_sums.at[g, halves[h]], slot, here.zhs[s], slot)
        elif g < 3:
            n, s = g - 1, ORDER[g]
            if h == n:
                waits["z_far", s]()
                z_sums[g, halves[h]] = z_sums[g, halves[h]] + z_far[n]
            slot = z_near.at[n, halves[h]]
            waits["z_near", s, h] = links.push(z_sums.at[g, halves[h]], slot, here.zhs[s], slot)

    blocks = [(0, 0), (0, 1), (1, 1), (2, 0), (1, 0), (2, 1), (3, 0), (3, 1)]
    x_first(blocks[0])
    x_first(blocks[1])
    for n, b in enumerate(blocks):
        x_second(b)
        if n + 2 < len(blocks):
            x_first(blocks[n + 2])
        if n >= 1:
            x_last(blocks[n - 1])
    x_last(blocks[-1])
    links.drain()
    for s, h in ((1, 1), (-1, 0), (1, 0), (-1, 1)):
        waits["z_near", s, h]()
    total = z_sums[3].astype(F32) + z_near[0].astype(F32) + z_near[1].astype(F32)
    return total.astype(BF16)


def gather_col(here, links, grads, between):
    rows = grads.shape[2]
    half = rows // 2
    piece = {1: pl.ds(0, half), -1: pl.ds(half, half)}
    last = []

    def at(x_off, z_off, k, where):
        return grads.at[here.chip_at(x_off, z_off), k, where]

    def to_core(x_off, z_off, where):
        mine = at(x_off, z_off, here.core, where)
        last.append(links.push(mine, mine, here.sibling, at(x_off, z_off, 1 - here.core, where)))

    def to_z(s, z_off, where):
        mine = at(0, z_off, here.core, where)
        return links.push(mine, mine, here.zhs[s], at(0, z_off - s, here.core, where))

    def to_x(s, x_off, z_off, where):
        mine = at(x_off, z_off, here.core, where)
        return links.push(mine, mine, here.xs[s], at(x_off - s, z_off, here.core, where))

    def cut(where):
        size = where.size // 2
        return {1: pl.ds(where.start, size), -1: pl.ds(where.start + size, size)}

    near, far = {}, {}

    def x_start(z_off, side):
        near[z_off, side] = {s: to_x(s, 0, z_off, piece[side]) for s in (1, -1)}

    def x_pass(z_off, side):
        far[z_off, side] = {}
        for s in (1, -1):
            near[z_off, side][s]()
            far[z_off, side][s] = to_x(s, -s, z_off, cut(piece[side])[s])
            to_core(-s, z_off, piece[side])

    def x_end(z_off, side):
        for s in (1, -1):
            far[z_off, side][s]()
            to_core(2, z_off, cut(piece[side])[s])

    first = {s: to_z(s, 0, piece[s]) for s in (1, -1)}
    second = {s: to_z(s, 0, piece[-s]) for s in (1, -1)}
    x_start(0, 1)
    x_start(0, -1)
    to_core(0, 0, pl.ds(0, rows))
    between()
    x_pass(0, 1)
    x_pass(0, -1)
    between()
    opposite = {}
    for s in (1, -1):
        first[s]()
        opposite[s] = to_z(s, -s, piece[s])
        x_start(-s, s)
        to_core(0, -s, piece[s])
    x_end(0, 1)
    x_end(0, -1)
    for s in (1, -1):
        x_pass(-s, s)
    for s in (1, -1):
        second[s]()
        x_start(-s, -s)
        to_core(0, -s, piece[-s])
    for s in (1, -1):
        x_end(-s, s)
    between()
    for s in (1, -1):
        x_pass(-s, -s)
    for s in (1, -1):
        opposite[s]()
        x_start(2, s)
        to_core(0, 2, piece[s])
    for s in (1, -1):
        x_end(-s, -s)
    between()
    for s in (1, -1):
        x_pass(2, s)
    for s in (1, -1):
        x_end(2, s)
    links.drain()
    for wait in last:
        wait()


def sum_row(here, links, part, a_in, a_sum, a_side, b_in, b_sum, b_side, between):
    rows = part.shape[2]
    far = here.rings // 2
    n_b = rows - SUM_PART
    part_a, part_b = pl.ds(0, SUM_PART), pl.ds(SUM_PART, n_b)
    waits = {}

    def half(count, cut, sign):
        return pl.ds(0, cut) if sign > 0 else pl.ds(cut, count - cut)

    def mine(y_off, z_off, where):
        index = here.row_at(y_off, z_off)
        return part[lax.div(index, 2), lax.rem(index, 2), where]

    def ring_send(key, hop, total, partial_in, sums):
        cut = SUM_CUTS[0] if key[0] == "A" else SUM_CUTS[1]
        count = partial_in.shape[2]
        for n, s in enumerate((1, -1)):
            at, slot = sums.at[n, hop - 1], partial_in.at[n, hop - 1]
            if hop == far:
                sums[n, hop - 1] = total(s)
                where = half(count, cut, s)
                at, slot = at.at[where], slot.at[where]
            elif hop + 1 == far:
                sums[n, hop - 1] = total(s)
                where = half(count, cut, s)
                waits[key, s]()
                sums[n, hop - 1, where] = sums[n, hop - 1, where] + partial_in[n, hop, where]
            else:
                own = total(s)
                waits[key, s]()
                sums[n, hop - 1] = own + partial_in[n, hop]
            waits[key, s] = links.push(at, slot, here.ys[s], slot)

    def ring_end(key, own, partial_in):
        for s in (1, -1):
            waits[key, s]()
        return own.astype(F32) + partial_in[0, 0].astype(F32) + partial_in[1, 0].astype(F32)

    def a_send(j, hop):
        ring_send(("A", j), hop, lambda s: mine(s * hop, j, part_a), a_in.at[j], a_sum.at[j])

    side_waits = []

    def a_across(j):
        a_side[0, j - 1] = ring_end(("A", j), mine(0, j, part_a), a_in.at[j]).astype(BF16)
        slot = a_side.at[1, j - 1]
        side_waits.append(links.push(a_side.at[0, j - 1], slot, here.zls[j], slot))

    offsets = [far] + [s * h for h in range(far - 1, 0, -1) for s in (1, -1)] + [0]
    b_waits = {}

    def b_across():
        for i, y_off in enumerate(offsets):
            b_waits[y_off] = []
            for j in range(1, Z_LO):
                slot = b_side.at[i, j - 1]
                source = chunk(part, here.row_at(y_off, j), part_b)
                b_waits[y_off].append(links.push(source, slot, here.zls[j], slot))

    def b_total(y_off):
        i = offsets.index(y_off)
        for wait in b_waits[y_off]:
            wait()
        b_waits[y_off] = []
        return mine(y_off, 0, part_b).astype(F32) + b_side[i, 0].astype(F32) + b_side[i, 1].astype(F32)

    def b_send(hop):
        ring_send(
            ("B", 0), hop, lambda s: b_total(far if hop == far else s * hop).astype(BF16), b_in, b_sum
        )

    a_send(1, far)
    a_send(2, far)
    b_across()
    a_send(0, far)
    between()
    for hop in range(far - 1, 0, -1):
        a_send(1, hop)
        a_send(2, hop)
        if hop + 2 <= far:
            b_send(hop + 2)
        if hop + 1 < far:
            a_send(0, hop + 1)
        between()
    a_across(1)
    a_across(2)
    b_send(2)
    a_send(0, 1)
    between()
    b_send(1)
    total_a = ring_end(("A", 0), mine(0, 0, part_a), a_in.at[0])
    total_b = ring_end(("B", 0), b_total(0), b_in)
    for j, wait in enumerate(side_waits):
        wait()
        total_a += a_side[1, j].astype(F32)
    return total_a.astype(BF16), total_b.astype(BF16)


def weight_sum(here, links, scale, w_half, w_out, w_core, w_y_out, w_y, w_x_out, w_x, w_lo, w_hi, w_all):
    core, y, x = here.core, here.y, here.x
    fine = w_x.shape[1]

    def pair():
        w_out[...] = w_half[1 - core].astype(BF16)
        return [links.push(w_out, w_core, here.sibling, w_core)]

    def over_y():
        w_half[core] = w_half[core] + w_core[...].astype(F32)
        w_y_out[...] = w_half[core].astype(BF16)
        return [
            links.push(w_y_out.at[wrap(y + j, here.rings)], w_y.at[j - 1], here.ys[j], w_y.at[j - 1])
            for j in range(1, here.rings)
        ]

    def over_x():
        total = w_half[core, y]
        for j in range(1, here.rings):
            total += w_y[j - 1].astype(F32)
        w_half[core, y] = total
        for i in range(here.n_x):
            w_x_out[i] = total[i * fine : (i + 1) * fine].astype(BF16)
        return [
            links.push(w_x_out.at[wrap(x + j, here.n_x)], w_x.at[j - 1], here.xs[j], w_x.at[j - 1])
            for j in range(1, here.n_x)
        ]

    def over_lo():
        total = w_half[core, y, pl.ds(x * fine, fine)]
        for j in range(1, here.n_x):
            total += w_x[j - 1].astype(F32)
        w_lo[here.zl] = total
        slot = w_lo.at[here.zl]
        return [links.push(slot, slot, here.zls[j], w_lo.at[wrap(here.zl - j, Z_LO)]) for j in range(1, Z_LO)]

    def over_hi():
        w_hi[here.zh] = w_lo[0] + w_lo[1] + w_lo[2]
        slot = w_hi.at[here.zh]
        return [links.push(slot, slot, here.zhs[j], w_hi.at[wrap(here.zh - j, Z_HI)]) for j in range(1, Z_HI)]

    def back_y():
        total = (w_hi[0] + w_hi[1]) + (w_hi[2] + w_hi[3])
        w_all[core, x, y] = (total * scale).astype(BF16)
        slot = w_all.at[core, x, y]
        return [
            links.push(slot, slot, here.ys[j], w_all.at[core, x, wrap(y - j, here.rings)])
            for j in range(1, here.rings)
        ]

    def back_x():
        slot = w_all.at[core, x]
        return [
            links.push(slot, slot, here.xs[j], w_all.at[core, wrap(x - j, here.n_x)])
            for j in range(1, here.n_x)
        ]

    def back_pair():
        return [links.push(w_all.at[core], w_all.at[core], here.sibling, w_all.at[1 - core])]

    return [pair, over_y, over_x, over_lo, over_hi, back_y, back_x, back_pair]


def kernel(
    rings,
    n_x,
    scale,
    live,
    tile_rows,
    tile_cols,
    feat_ref,
    tiles_ref,
    weight_ref,
    cot_ref,
    hidden_ref,
    grad_feat_ref,
    grad_weight_ref,
    tiles,
    feats,
    total,
    part,
    from_core,
    sums,
    x_far,
    x_near,
    z_sums,
    z_far,
    z_near,
    grads,
    back,
    a_in,
    a_sum,
    a_side,
    b_in,
    b_sum,
    b_side,
    w_half,
    w_out,
    w_core,
    w_y_out,
    w_y,
    w_x_out,
    w_x,
    w_lo,
    w_hi,
    w_all,
    send,
    recv,
    local,
):
    here = Place(rings, n_x)
    links = Links(send, recv)
    load = pltpu.make_async_copy(tiles_ref, tiles, local)
    load.start()
    feats[lax.div(here.row, 2), lax.rem(here.row, 2)] = feat_ref[...]
    here.greet()
    gather_row(here, links, feats)
    load.wait()
    tile_products(tiles, feats, tile_rows, tile_cols, total, False)
    own_sum = sum_col(
        here,
        links,
        lambda target: target_sum(total, tile_rows, live, target),
        part,
        from_core,
        sums,
        x_far,
        x_near,
        z_sums,
        z_far,
        z_near,
    )
    pre_act = jnp.dot(own_sum, weight_ref[...], preferred_element_type=F32)
    gate = jax.nn.sigmoid(pre_act)
    own_grad = (cot_ref[...].astype(F32) * gate * (1.0 + pre_act * (1.0 - gate))).astype(BF16)
    grads[here.chip, here.core] = own_grad

    stages = weight_sum(
        here, links, scale, w_half, w_out, w_core, w_y_out, w_y, w_x_out, w_x, w_lo, w_hi, w_all
    )
    weight_waits = []

    def weight_step():
        for wait in weight_waits:
            wait()
        del weight_waits[:]
        if stages:
            weight_waits.extend(stages.pop(0)())

    def beside_gather():
        if len(stages) == 8:
            hidden_ref[...] = (pre_act * gate).astype(hidden_ref.dtype)
            term = lax.dot_general(own_sum, own_grad, (((0,), (0,)), ((), ())), preferred_element_type=F32)
            columns = term.shape[1] // 2
            for k in range(2):
                w_half[k] = term[:, k * columns : (k + 1) * columns].reshape(w_half.shape[1:])
        weight_step()

    gather_col(here, links, grads, beside_gather)
    tile_products(tiles, grads, tile_cols, tile_rows, total, True)
    rows, width = back.shape[2:]

    def store(target, _):
        back[target] = target_sum(total, tile_cols, live, target).astype(BF16).reshape(2, rows, width)
        return 0

    lax.fori_loop(0, back.shape[0], store, 0)
    parts = sum_row(here, links, back, a_in, a_sum, a_side, b_in, b_sum, b_side, weight_step)
    low = 0
    for chunk_sum in parts:
        count = chunk_sum.shape[0]
        grad_feat_ref[pl.ds(low, count)] = lax.dot_general(
            chunk_sum, weight_ref[...], (((1,), (1,)), ((), ())), preferred_element_type=F32
        ).astype(grad_feat_ref.dtype)
        low += count
    while stages or weight_waits:
        weight_step()
    columns = w_all.shape[-1]
    for k in range(2):
        for i in range(n_x):
            grad_weight_ref[:, i, :, k * columns : (k + 1) * columns] = w_all[k, i].astype(F32)
    links.drain()


def shards(features, tile_values, tile_rows, tile_cols, tile_live, weight, cotangent):
    rows, width = features.shape
    slots, edge, _ = tile_values.shape
    n_row, n_col = lax.axis_size("row"), lax.axis_size("col")
    rings, n_x = n_row // Z_LO, n_col // (2 * Z_HI)
    far, n_b = rings // 2, rows - SUM_PART
    columns, coarse = width // 2, width // rings
    fine = coarse // n_x
    vmem = pl.BlockSpec(memory_space=pltpu.VMEM)
    smem = pl.BlockSpec(memory_space=pltpu.SMEM)
    scratch = [
        pltpu.VMEM(shape, dtype)
        for shape, dtype in (
            ((slots, edge, edge), BF16),
            ((n_row // 2, 2, rows, width), BF16),
            ((slots + 1, edge, width), F32),
            ((n_col // 2, 2, rows, width), BF16),
            ((4, 4, rows, width), BF16),
            ((4, 4, rows, width), BF16),
            ((4, 2, 2, rows // 4, width), BF16),
            ((4, 2, 2, rows // 2, width), BF16),
            ((4, rows, width), BF16),
            ((2, rows // 2, width), BF16),
            ((2, rows, width), BF16),
            ((n_col // 2, 2, rows, width), BF16),
            ((n_row // 2, 2, rows, width), BF16),
            ((Z_LO, 2, far, SUM_PART, width), BF16),
            ((Z_LO, 2, far, SUM_PART, width), BF16),
            ((2, Z_LO - 1, SUM_PART, width), BF16),
            ((2, far, n_b, width), BF16),
            ((2, far, n_b, width), BF16),
            ((rings, Z_LO - 1, n_b, width), BF16),
            ((2, rings, coarse, columns), F32),
            ((rings, coarse, columns), BF16),
            ((rings, coarse, columns), BF16),
            ((rings, coarse, columns), BF16),
            ((rings - 1, coarse, columns), BF16),
            ((n_x, fine, columns), BF16),
            ((n_x - 1, fine, columns), BF16),
            ((Z_LO, fine, columns), F32),
            ((Z_HI, fine, columns), F32),
            ((2, n_x, rings, fine, columns), BF16),
        )
    ]
    hidden, grad_features, grad_weight = pl.pallas_call(
        functools.partial(kernel, rings, n_x, float(rows * n_row * n_col) ** -0.5),
        out_shape=(
            jax.ShapeDtypeStruct((rows, width), BF16),
            jax.ShapeDtypeStruct((rows, width), BF16),
            jax.ShapeDtypeStruct((rings, n_x, fine, width), F32),
        ),
        in_specs=[smem, smem, smem, vmem, pl.BlockSpec(memory_space=pl.ANY), vmem, vmem],
        out_specs=(vmem, vmem, vmem),
        scratch_shapes=scratch
        + [
            pltpu.SemaphoreType.DMA((320,)),
            pltpu.SemaphoreType.DMA((320,)),
            pltpu.SemaphoreType.DMA,
        ],
        compiler_params=pltpu.CompilerParams(
            collective_id=0, has_side_effects=True, vmem_limit_bytes=VMEM_LIMIT
        ),
        name="graph_layer",
    )(tile_live, tile_rows, tile_cols, features, tile_values, weight, cotangent)
    return hidden, grad_features, grad_weight.reshape(width, width)


def solution(mesh):
    return jax.shard_map(
        shards,
        mesh=mesh,
        in_specs=(
            P(("col", "row"), None),
            P(("row", "col"), None, None),
            P(("row", "col")),
            P(("row", "col")),
            P(("row", "col")),
            P(),
            P(("row", "col"), None),
        ),
        out_specs=(P(("row", "col"), None), P(("col", "row"), None), P()),
        check_vma=False,
    )
```

```python
import functools

import jax
import jax.numpy as jnp
from jax import lax
from jax.experimental import pallas as pl
from jax.experimental.pallas import tpu as pltpu
from jax.sharding import PartitionSpec as P

MESH = pl.DeviceIdType.MESH
F32 = jnp.float32
BF16 = jnp.bfloat16
Z_LO = 3
Z_HI = 4
VMEM_LIMIT = 46 * 1024 * 1024
GATHER_PART, GATHER_CUTS = 64, (32, 32)
SUM_PART, SUM_CUTS = 80, (48, 16)


def wrap(value, size):
    return lax.rem(value + 2 * size, size)


class Links:
    def __init__(self, send, recv):
        self.send, self.recv, self.count, self.sent = send, recv, 0, []

    def push(self, src, dst, peer, lands):
        i = self.count
        self.count += 1

        def copy(source, target):
            return pltpu.make_async_remote_copy(
                src_ref=source,
                dst_ref=target,
                send_sem=self.send.at[i],
                recv_sem=self.recv.at[i],
                device_id=peer,
                device_id_type=MESH,
            )

        out = copy(src, dst)
        out.start()
        self.sent.append(out)
        return copy(lands, lands).wait_recv

    def drain(self):
        for copy in self.sent:
            copy.wait_send()
        self.sent = []


class Place:
    def __init__(self, rings, n_x):
        self.rings, self.n_x = rings, n_x
        self.row, self.col = lax.axis_index("row"), lax.axis_index("col")
        self.y, self.zl = lax.div(self.row, Z_LO), lax.rem(self.row, Z_LO)
        self.chip, self.core = lax.div(self.col, 2), lax.rem(self.col, 2)
        self.x, self.zh = lax.div(self.chip, Z_HI), lax.rem(self.chip, Z_HI)
        self.sibling = {"col": self.chip * 2 + 1 - self.core}
        self.xs = {j: {"col": self.chip_at(j, 0) * 2 + self.core} for j in range(1, n_x)}
        self.zhs = {j: {"col": self.chip_at(0, j) * 2 + self.core} for j in range(1, Z_HI)}
        self.ys = {j: {"row": self.row_at(j, 0)} for j in range(1, rings)}
        self.zls = {j: {"row": self.row_at(0, j)} for j in range(1, Z_LO)}
        for peers, size in ((self.xs, n_x), (self.zhs, Z_HI), (self.ys, rings), (self.zls, Z_LO)):
            peers[-1] = peers[size - 1]

    def chip_at(self, x_off, z_off):
        return wrap(self.x + x_off, self.n_x) * Z_HI + wrap(self.zh + z_off, Z_HI)

    def row_at(self, y_off, z_off):
        return wrap(self.y + y_off, self.rings) * Z_LO + wrap(self.zl + z_off, Z_LO)

    def greet(self):
        barrier = pltpu.get_barrier_semaphore()
        peers = [self.sibling]
        for group in (self.xs, self.zhs, self.ys, self.zls):
            peers += [peer for j, peer in group.items() if j > 0]
        for peer in peers:
            pl.semaphore_signal(barrier, inc=1, device_id=peer, device_id_type=MESH)
        pl.semaphore_wait(barrier, len(peers))


def chunk(ref, index, rows=None):
    at = ref.at[lax.div(index, 2), lax.rem(index, 2)]
    return at if rows is None else at.at[rows]


def gather_row(here, links, buf):
    rows = buf.shape[2]
    far = here.rings // 2
    parts = {"B": (GATHER_PART, rows - GATHER_PART, GATHER_CUTS[1])}
    for j in range(Z_LO):
        parts[j] = (0, GATHER_PART, GATHER_CUTS[0])

    def span(tag, sign, hop):
        low, count, cut = parts[tag]
        if hop < far:
            return pl.ds(low, count)
        return pl.ds(low, cut) if sign > 0 else pl.ds(low + cut, count - cut)

    def ring(tag, sign, hop):
        where = span(tag, sign, hop)
        z_off = 0 if tag == "B" else -tag
        mine = chunk(buf, here.row_at(-sign * (hop - 1), z_off), where)
        theirs = chunk(buf, here.row_at(-sign * hop, z_off), where)
        return links.push(mine, mine, here.ys[sign], theirs)

    def side(y_off, where):
        waits = []
        for j in range(1, Z_LO):
            mine = chunk(buf, here.row_at(y_off, 0), where)
            theirs = chunk(buf, here.row_at(y_off, -j), where)
            waits.append(links.push(mine, mine, here.zls[j], theirs))
        return waits

    pending, last = {}, []

    def launch(tag):
        for sign in (1, -1):
            pending[tag, sign] = ring(tag, sign, 1)

    def step(tag, hop):
        for sign in (1, -1):
            pending[tag, sign]()
            if hop < far:
                pending[tag, sign] = ring(tag, sign, hop + 1)
            if tag == "B":
                last.extend(side(-sign * hop, span(tag, sign, hop)))

    launch("B")
    launch(0)
    first = side(0, span(0, 1, 1))
    last.extend(side(0, span("B", 1, 1)))
    step("B", 1)
    step(0, 1)
    for j in range(1, Z_LO):
        first[j - 1]()
        launch(j)
    for hop in range(2, far + 1):
        step("B", hop)
        step(0, hop)
        for j in range(1, Z_LO):
            step(j, hop - 1)
    for j in range(1, Z_LO):
        step(j, far)
    for wait in last:
        wait()


def tile_products(tiles, source, into, origin, total, transposed):
    slots = tiles.shape[0]
    total[slots] = jnp.zeros(total.shape[1:], F32)

    def slot(k, _):
        before = jnp.int32(slots)
        for j in range(slots):
            before = jnp.where((j < k) & (into[j] == into[k]), j, before)
        block = source[origin[k]]
        total[k] = total[before] + lax.dot_general(
            tiles[k],
            block.reshape(block.shape[0] * block.shape[1], block.shape[2]),
            (((0 if transposed else 1,), (0,)), ((), ())),
            preferred_element_type=F32,
        )
        return 0

    lax.fori_loop(0, slots, slot, 0)


def target_sum(total, into, live, target):
    slots = total.shape[0] - 1
    count = live[0]
    last = jnp.int32(slots)
    for j in range(slots):
        last = jnp.where((j < count) & (into[j] == target), j, last)
    return total[last]


ORDER = (2, 1, -1, 0)


def sum_col(here, links, tile, part, from_core, sums, x_far, x_near, z_sums, z_far, z_near):
    rows, width = part.shape[2:]
    half, quarter = rows // 2, rows // 4
    halves = (pl.ds(0, half), pl.ds(half, half))
    core = here.core
    arrived = {}
    for g, z_off in enumerate(ORDER):
        for i, x_off in enumerate(ORDER):
            chip = here.chip_at(x_off, z_off)
            part[chip] = tile(chip).astype(BF16).reshape(2, rows, width)
            slot = from_core.at[g, i]
            arrived[g, i] = links.push(part.at[chip, 1 - core], slot, here.sibling, slot)

    def pair_sum(g, i):
        if (g, i) in arrived:
            arrived.pop((g, i))()
            sums[g, i] = part[here.chip_at(ORDER[i], ORDER[g]), core] + from_core[g, i]

    def quarter_of(h, s):
        return pl.ds(h * half + (0 if s > 0 else quarter), quarter)

    waits = {}

    def x_first(b):
        g, h = b
        pair_sum(g, 0)
        for n, s in enumerate((1, -1)):
            slot = x_far.at[g, h, n]
            waits[b, "far", s] = links.push(sums.at[g, 0, quarter_of(h, s)], slot, here.xs[s], slot)

    def x_second(b):
        g, h = b
        for n, s in enumerate((1, -1)):
            pair_sum(g, 1 + n)
            waits[b, "far", s]()
            where = quarter_of(h, s)
            sums[g, 1 + n, where] = sums[g, 1 + n, where] + x_far[g, h, n]
            slot = x_near.at[g, h, n]
            waits[b, "near", s] = links.push(sums.at[g, 1 + n, halves[h]], slot, here.xs[s], slot)

    def x_last(b):
        g, h = b
        pair_sum(g, 3)
        for s in (1, -1):
            waits[b, "near", s]()
        total = sums[g, 3, halves[h]].astype(F32) + x_near[g, h, 0].astype(F32) + x_near[g, h, 1].astype(F32)
        z_sums[g, halves[h]] = total.astype(BF16)
        if g == 0:
            n, s = h, (1, -1)[h]
            slot = z_far.at[n]
            waits["z_far", s] = links.push(z_sums.at[g, halves[h]], slot, here.zhs[s], slot)
        elif g < 3:
            n, s = g - 1, ORDER[g]
            if h == n:
                waits["z_far", s]()
                z_sums[g, halves[h]] = z_sums[g, halves[h]] + z_far[n]
            slot = z_near.at[n, halves[h]]
            waits["z_near", s, h] = links.push(z_sums.at[g, halves[h]], slot, here.zhs[s], slot)

    blocks = [(0, 0), (0, 1), (1, 1), (2, 0), (1, 0), (2, 1), (3, 0), (3, 1)]
    x_first(blocks[0])
    x_first(blocks[1])
    for n, b in enumerate(blocks):
        x_second(b)
        if n + 2 < len(blocks):
            x_first(blocks[n + 2])
        if n >= 1:
            x_last(blocks[n - 1])
    x_last(blocks[-1])
    links.drain()
    for s, h in ((1, 1), (-1, 0), (1, 0), (-1, 1)):
        waits["z_near", s, h]()
    total = z_sums[3].astype(F32) + z_near[0].astype(F32) + z_near[1].astype(F32)
    return total.astype(BF16)


def gather_col(here, links, grads, between):
    rows = grads.shape[2]
    half = rows // 2
    piece = {1: pl.ds(0, half), -1: pl.ds(half, half)}
    last = []

    def at(x_off, z_off, k, where):
        return grads.at[here.chip_at(x_off, z_off), k, where]

    def to_core(x_off, z_off, where):
        mine = at(x_off, z_off, here.core, where)
        last.append(links.push(mine, mine, here.sibling, at(x_off, z_off, 1 - here.core, where)))

    def to_z(s, z_off, where):
        mine = at(0, z_off, here.core, where)
        return links.push(mine, mine, here.zhs[s], at(0, z_off - s, here.core, where))

    def to_x(s, x_off, z_off, where):
        mine = at(x_off, z_off, here.core, where)
        return links.push(mine, mine, here.xs[s], at(x_off - s, z_off, here.core, where))

    def cut(where):
        size = where.size // 2
        return {1: pl.ds(where.start, size), -1: pl.ds(where.start + size, size)}

    near, far = {}, {}

    def x_start(z_off, side):
        near[z_off, side] = {s: to_x(s, 0, z_off, piece[side]) for s in (1, -1)}

    def x_pass(z_off, side):
        far[z_off, side] = {}
        for s in (1, -1):
            near[z_off, side][s]()
            far[z_off, side][s] = to_x(s, -s, z_off, cut(piece[side])[s])
            to_core(-s, z_off, piece[side])

    def x_end(z_off, side):
        for s in (1, -1):
            far[z_off, side][s]()
            to_core(2, z_off, cut(piece[side])[s])

    first = {s: to_z(s, 0, piece[s]) for s in (1, -1)}
    second = {s: to_z(s, 0, piece[-s]) for s in (1, -1)}
    x_start(0, 1)
    x_start(0, -1)
    to_core(0, 0, pl.ds(0, rows))
    between()
    x_pass(0, 1)
    x_pass(0, -1)
    between()
    opposite = {}
    for s in (1, -1):
        first[s]()
        opposite[s] = to_z(s, -s, piece[s])
        x_start(-s, s)
        to_core(0, -s, piece[s])
    x_end(0, 1)
    x_end(0, -1)
    for s in (1, -1):
        x_pass(-s, s)
    for s in (1, -1):
        second[s]()
        x_start(-s, -s)
        to_core(0, -s, piece[-s])
    for s in (1, -1):
        x_end(-s, s)
    between()
    for s in (1, -1):
        x_pass(-s, -s)
    for s in (1, -1):
        opposite[s]()
        x_start(2, s)
        to_core(0, 2, piece[s])
    for s in (1, -1):
        x_end(-s, -s)
    between()
    for s in (1, -1):
        x_pass(2, s)
    between()
    for s in (1, -1):
        x_end(2, s)
    links.drain()
    for wait in last:
        wait()


def sum_row(here, links, part, a_in, a_sum, a_side, b_in, b_sum, b_side, between):
    rows = part.shape[2]
    far = here.rings // 2
    n_b = rows - SUM_PART
    part_a, part_b = pl.ds(0, SUM_PART), pl.ds(SUM_PART, n_b)
    waits = {}

    def half(count, cut, sign):
        return pl.ds(0, cut) if sign > 0 else pl.ds(cut, count - cut)

    def mine(y_off, z_off, where):
        index = here.row_at(y_off, z_off)
        return part[lax.div(index, 2), lax.rem(index, 2), where]

    def ring_send(key, hop, total, partial_in, sums):
        cut = SUM_CUTS[0] if key[0] == "A" else SUM_CUTS[1]
        count = partial_in.shape[2]
        for n, s in enumerate((1, -1)):
            at, slot = sums.at[n, hop - 1], partial_in.at[n, hop - 1]
            if hop == far:
                sums[n, hop - 1] = total(s)
                where = half(count, cut, s)
                at, slot = at.at[where], slot.at[where]
            elif hop + 1 == far:
                sums[n, hop - 1] = total(s)
                where = half(count, cut, s)
                waits[key, s]()
                sums[n, hop - 1, where] = sums[n, hop - 1, where] + partial_in[n, hop, where]
            else:
                own = total(s)
                waits[key, s]()
                sums[n, hop - 1] = own + partial_in[n, hop]
            waits[key, s] = links.push(at, slot, here.ys[s], slot)

    def ring_end(key, own, partial_in):
        for s in (1, -1):
            waits[key, s]()
        return own.astype(F32) + partial_in[0, 0].astype(F32) + partial_in[1, 0].astype(F32)

    def a_send(j, hop):
        ring_send(("A", j), hop, lambda s: mine(s * hop, j, part_a), a_in.at[j], a_sum.at[j])

    side_waits = []

    def a_across(j):
        a_side[0, j - 1] = ring_end(("A", j), mine(0, j, part_a), a_in.at[j]).astype(BF16)
        slot = a_side.at[1, j - 1]
        side_waits.append(links.push(a_side.at[0, j - 1], slot, here.zls[j], slot))

    offsets = [far] + [s * h for h in range(far - 1, 0, -1) for s in (1, -1)] + [0]
    b_waits = {}

    def b_across():
        for i, y_off in enumerate(offsets):
            b_waits[y_off] = []
            for j in range(1, Z_LO):
                slot = b_side.at[i, j - 1]
                source = chunk(part, here.row_at(y_off, j), part_b)
                b_waits[y_off].append(links.push(source, slot, here.zls[j], slot))

    def b_total(y_off):
        i = offsets.index(y_off)
        for wait in b_waits[y_off]:
            wait()
        b_waits[y_off] = []
        return mine(y_off, 0, part_b).astype(F32) + b_side[i, 0].astype(F32) + b_side[i, 1].astype(F32)

    def b_send(hop):
        ring_send(
            ("B", 0), hop, lambda s: b_total(far if hop == far else s * hop).astype(BF16), b_in, b_sum
        )

    a_send(1, far)
    a_send(2, far)
    b_across()
    a_send(0, far)
    between()
    for hop in range(far - 1, 0, -1):
        a_send(1, hop)
        a_send(2, hop)
        if hop + 2 <= far:
            b_send(hop + 2)
        if hop + 1 < far:
            a_send(0, hop + 1)
        between()
    a_across(1)
    a_across(2)
    b_send(2)
    a_send(0, 1)
    between()
    b_send(1)
    total_a = ring_end(("A", 0), mine(0, 0, part_a), a_in.at[0])
    total_b = ring_end(("B", 0), b_total(0), b_in)
    for j, wait in enumerate(side_waits):
        wait()
        total_a += a_side[1, j].astype(F32)
    return total_a.astype(BF16), total_b.astype(BF16)


def weight_sum(here, links, scale, w_half, w_out, w_core, w_y_out, w_y, w_x_out, w_x, w_lo, w_hi, w_all):
    core, y, x = here.core, here.y, here.x
    fine = w_x.shape[1]

    def pair():
        w_out[...] = w_half[1 - core].astype(BF16)
        return [links.push(w_out, w_core, here.sibling, w_core)]

    def over_y():
        w_half[core] = w_half[core] + w_core[...].astype(F32)
        w_y_out[...] = w_half[core].astype(BF16)
        return [
            links.push(w_y_out.at[wrap(y + j, here.rings)], w_y.at[j - 1], here.ys[j], w_y.at[j - 1])
            for j in range(1, here.rings)
        ]

    def over_x():
        total = w_half[core, y]
        for j in range(1, here.rings):
            total += w_y[j - 1].astype(F32)
        w_half[core, y] = total
        for i in range(here.n_x):
            w_x_out[i] = total[i * fine : (i + 1) * fine].astype(BF16)
        return [
            links.push(w_x_out.at[wrap(x + j, here.n_x)], w_x.at[j - 1], here.xs[j], w_x.at[j - 1])
            for j in range(1, here.n_x)
        ]

    def over_lo():
        total = w_half[core, y, pl.ds(x * fine, fine)]
        for j in range(1, here.n_x):
            total += w_x[j - 1].astype(F32)
        w_lo[here.zl] = total
        slot = w_lo.at[here.zl]
        return [links.push(slot, slot, here.zls[j], w_lo.at[wrap(here.zl - j, Z_LO)]) for j in range(1, Z_LO)]

    def over_hi():
        w_hi[here.zh] = w_lo[0] + w_lo[1] + w_lo[2]
        slot = w_hi.at[here.zh]
        return [links.push(slot, slot, here.zhs[j], w_hi.at[wrap(here.zh - j, Z_HI)]) for j in range(1, Z_HI)]

    def back_y():
        total = (w_hi[0] + w_hi[1]) + (w_hi[2] + w_hi[3])
        w_all[core, x, y] = (total * scale).astype(BF16)
        slot = w_all.at[core, x, y]
        return [
            links.push(slot, slot, here.ys[j], w_all.at[core, x, wrap(y - j, here.rings)])
            for j in range(1, here.rings)
        ]

    def back_x():
        slot = w_all.at[core, x]
        return [
            links.push(slot, slot, here.xs[j], w_all.at[core, wrap(x - j, here.n_x)])
            for j in range(1, here.n_x)
        ]

    def back_pair():
        return [links.push(w_all.at[core], w_all.at[core], here.sibling, w_all.at[1 - core])]

    return [pair, over_y, over_x, over_lo, over_hi, back_y, back_x, back_pair]


def kernel(
    rings,
    n_x,
    scale,
    live,
    tile_rows,
    tile_cols,
    feat_ref,
    tiles_ref,
    weight_ref,
    cot_ref,
    hidden_ref,
    grad_feat_ref,
    grad_weight_ref,
    weight,
    cot,
    tiles,
    feats,
    total,
    part,
    from_core,
    sums,
    x_far,
    x_near,
    z_sums,
    z_far,
    z_near,
    grads,
    back,
    a_in,
    a_sum,
    a_side,
    b_in,
    b_sum,
    b_side,
    w_half,
    w_out,
    w_core,
    w_y_out,
    w_y,
    w_x_out,
    w_x,
    w_lo,
    w_hi,
    w_all,
    send,
    recv,
    local,
):
    here = Place(rings, n_x)
    links = Links(send, recv)
    loads = [
        pltpu.make_async_copy(source, target, local.at[i])
        for i, (source, target) in enumerate(
            (
                (feat_ref, chunk(feats, here.row)),
                (tiles_ref, tiles),
                (weight_ref, weight),
                (cot_ref, cot),
            )
        )
    ]
    for load in loads:
        load.start()
    here.greet()
    loads[0].wait()
    gather_row(here, links, feats)
    for load in loads[1:]:
        load.wait()
    tile_products(tiles, feats, tile_rows, tile_cols, total, False)
    own_sum = sum_col(
        here,
        links,
        lambda target: target_sum(total, tile_rows, live, target),
        part,
        from_core,
        sums,
        x_far,
        x_near,
        z_sums,
        z_far,
        z_near,
    )
    pre_act = jnp.dot(own_sum, weight[...], preferred_element_type=F32)
    gate = jax.nn.sigmoid(pre_act)
    own_grad = (cot[...].astype(F32) * gate * (1.0 + pre_act * (1.0 - gate))).astype(BF16)
    grads[here.chip, here.core] = own_grad

    stages = weight_sum(
        here, links, scale, w_half, w_out, w_core, w_y_out, w_y, w_x_out, w_x, w_lo, w_hi, w_all
    )
    weight_waits = []

    def weight_step():
        for wait in weight_waits:
            wait()
        del weight_waits[:]
        if stages:
            weight_waits.extend(stages.pop(0)())

    def beside_gather():
        if len(stages) == 8:
            hidden_ref[...] = (pre_act * gate).astype(hidden_ref.dtype)
            term = lax.dot_general(own_sum, own_grad, (((0,), (0,)), ((), ())), preferred_element_type=F32)
            columns = term.shape[1] // 2
            for k in range(2):
                w_half[k] = term[:, k * columns : (k + 1) * columns].reshape(w_half.shape[1:])
        weight_step()

    gather_col(here, links, grads, beside_gather)
    weight_step()
    tile_products(tiles, grads, tile_cols, tile_rows, total, True)
    weight_step()
    rows, width = back.shape[2:]

    def store(target, _):
        back[target] = target_sum(total, tile_cols, live, target).astype(BF16).reshape(2, rows, width)
        return 0

    lax.fori_loop(0, back.shape[0], store, 0)
    parts = sum_row(here, links, back, a_in, a_sum, a_side, b_in, b_sum, b_side, weight_step)
    low = 0
    for chunk_sum in parts:
        count = chunk_sum.shape[0]
        grad_feat_ref[pl.ds(low, count)] = lax.dot_general(
            chunk_sum, weight[...], (((1,), (1,)), ((), ())), preferred_element_type=F32
        ).astype(grad_feat_ref.dtype)
        low += count
    while stages or weight_waits:
        weight_step()
    columns = w_all.shape[-1]
    for k in range(2):
        for i in range(n_x):
            grad_weight_ref[:, i, :, k * columns : (k + 1) * columns] = w_all[k, i].astype(F32)
    links.drain()


def shards(features, tile_values, tile_rows, tile_cols, tile_live, weight, cotangent):
    rows, width = features.shape
    slots, edge, _ = tile_values.shape
    n_row, n_col = lax.axis_size("row"), lax.axis_size("col")
    rings, n_x = n_row // Z_LO, n_col // (2 * Z_HI)
    far, n_b = rings // 2, rows - SUM_PART
    columns, coarse = width // 2, width // rings
    fine = coarse // n_x
    vmem = pl.BlockSpec(memory_space=pltpu.VMEM)
    smem = pl.BlockSpec(memory_space=pltpu.SMEM)
    scratch = [
        pltpu.VMEM(shape, dtype)
        for shape, dtype in (
            ((width, width), BF16),
            ((rows, width), BF16),
            ((slots, edge, edge), BF16),
            ((n_row // 2, 2, rows, width), BF16),
            ((slots + 1, edge, width), F32),
            ((n_col // 2, 2, rows, width), BF16),
            ((4, 4, rows, width), BF16),
            ((4, 4, rows, width), BF16),
            ((4, 2, 2, rows // 4, width), BF16),
            ((4, 2, 2, rows // 2, width), BF16),
            ((4, rows, width), BF16),
            ((2, rows // 2, width), BF16),
            ((2, rows, width), BF16),
            ((n_col // 2, 2, rows, width), BF16),
            ((n_row // 2, 2, rows, width), BF16),
            ((Z_LO, 2, far, SUM_PART, width), BF16),
            ((Z_LO, 2, far, SUM_PART, width), BF16),
            ((2, Z_LO - 1, SUM_PART, width), BF16),
            ((2, far, n_b, width), BF16),
            ((2, far, n_b, width), BF16),
            ((rings, Z_LO - 1, n_b, width), BF16),
            ((2, rings, coarse, columns), F32),
            ((rings, coarse, columns), BF16),
            ((rings, coarse, columns), BF16),
            ((rings, coarse, columns), BF16),
            ((rings - 1, coarse, columns), BF16),
            ((n_x, fine, columns), BF16),
            ((n_x - 1, fine, columns), BF16),
            ((Z_LO, fine, columns), F32),
            ((Z_HI, fine, columns), F32),
            ((2, n_x, rings, fine, columns), BF16),
        )
    ]
    hidden, grad_features, grad_weight = pl.pallas_call(
        functools.partial(kernel, rings, n_x, float(rows * n_row * n_col) ** -0.5),
        out_shape=(
            jax.ShapeDtypeStruct((rows, width), BF16),
            jax.ShapeDtypeStruct((rows, width), BF16),
            jax.ShapeDtypeStruct((rings, n_x, fine, width), F32),
        ),
        in_specs=[smem] * 3 + [pl.BlockSpec(memory_space=pl.ANY)] * 4,
        out_specs=(vmem, vmem, vmem),
        scratch_shapes=scratch
        + [
            pltpu.SemaphoreType.DMA((320,)),
            pltpu.SemaphoreType.DMA((320,)),
            pltpu.SemaphoreType.DMA((4,)),
        ],
        compiler_params=pltpu.CompilerParams(
            collective_id=0, has_side_effects=True, vmem_limit_bytes=VMEM_LIMIT
        ),
        name="graph_layer",
    )(tile_live, tile_rows, tile_cols, features, tile_values, weight, cotangent)
    return hidden, grad_features, grad_weight.reshape(width, width)


def solution(mesh):
    return jax.shard_map(
        shards,
        mesh=mesh,
        in_specs=(
            P(("col", "row"), None),
            P(("row", "col"), None, None),
            P(("row", "col")),
            P(("row", "col")),
            P(("row", "col")),
            P(),
            P(("row", "col"), None),
        ),
        out_specs=(P(("row", "col"), None), P(("col", "row"), None), P()),
        check_vma=False,
    )
```

```python
import functools

import jax
import jax.numpy as jnp
from jax import lax
from jax.experimental import pallas as pl
from jax.experimental.pallas import tpu as pltpu
from jax.sharding import PartitionSpec as P

MESH = pl.DeviceIdType.MESH
F32 = jnp.float32
BF16 = jnp.bfloat16
Z_LO = 3
Z_HI = 4
VMEM_LIMIT = 56 * 1024 * 1024
GATHER_PART, GATHER_CUTS = 64, (32, 32)
SUM_PART, SUM_CUTS = 80, (48, 16)


def wrap(value, size):
    return lax.rem(value + 2 * size, size)


class Links:
    def __init__(self, send, recv):
        self.send, self.recv, self.count, self.sent = send, recv, 0, []

    def push(self, src, dst, peer, lands):
        i = self.count
        self.count += 1

        def copy(source, target):
            return pltpu.make_async_remote_copy(
                src_ref=source,
                dst_ref=target,
                send_sem=self.send.at[i],
                recv_sem=self.recv.at[i],
                device_id=peer,
                device_id_type=MESH,
            )

        out = copy(src, dst)
        out.start()
        self.sent.append(out)
        return copy(lands, lands).wait_recv

    def drain(self):
        for copy in self.sent:
            copy.wait_send()
        self.sent = []


class Place:
    def __init__(self, rings, n_x):
        self.rings, self.n_x = rings, n_x
        self.row, self.col = lax.axis_index("row"), lax.axis_index("col")
        self.y, self.zl = lax.div(self.row, Z_LO), lax.rem(self.row, Z_LO)
        self.chip, self.core = lax.div(self.col, 2), lax.rem(self.col, 2)
        self.x, self.zh = lax.div(self.chip, Z_HI), lax.rem(self.chip, Z_HI)
        self.sibling = {"col": self.chip * 2 + 1 - self.core}
        self.xs = {j: {"col": self.chip_at(j, 0) * 2 + self.core} for j in range(1, n_x)}
        self.zhs = {j: {"col": self.chip_at(0, j) * 2 + self.core} for j in range(1, Z_HI)}
        self.ys = {j: {"row": self.row_at(j, 0)} for j in range(1, rings)}
        self.zls = {j: {"row": self.row_at(0, j)} for j in range(1, Z_LO)}
        for peers, size in ((self.xs, n_x), (self.zhs, Z_HI), (self.ys, rings), (self.zls, Z_LO)):
            peers[-1] = peers[size - 1]

    def chip_at(self, x_off, z_off):
        return wrap(self.x + x_off, self.n_x) * Z_HI + wrap(self.zh + z_off, Z_HI)

    def row_at(self, y_off, z_off):
        return wrap(self.y + y_off, self.rings) * Z_LO + wrap(self.zl + z_off, Z_LO)

    def greet(self):
        barrier = pltpu.get_barrier_semaphore()
        peers = [self.sibling]
        for group in (self.xs, self.zhs, self.ys, self.zls):
            peers += [peer for j, peer in group.items() if j > 0]
        for peer in peers:
            pl.semaphore_signal(barrier, inc=1, device_id=peer, device_id_type=MESH)
        pl.semaphore_wait(barrier, len(peers))


def chunk(ref, index, rows=None):
    at = ref.at[lax.div(index, 2), lax.rem(index, 2)]
    return at if rows is None else at.at[rows]


def gather_row(here, links, buf):
    rows = buf.shape[2]
    far = here.rings // 2
    parts = {"B": (GATHER_PART, rows - GATHER_PART, GATHER_CUTS[1])}
    for j in range(Z_LO):
        parts[j] = (0, GATHER_PART, GATHER_CUTS[0])

    def span(tag, sign, hop):
        low, count, cut = parts[tag]
        if hop < far:
            return pl.ds(low, count)
        return pl.ds(low, cut) if sign > 0 else pl.ds(low + cut, count - cut)

    def ring(tag, sign, hop):
        where = span(tag, sign, hop)
        z_off = 0 if tag == "B" else -tag
        mine = chunk(buf, here.row_at(-sign * (hop - 1), z_off), where)
        theirs = chunk(buf, here.row_at(-sign * hop, z_off), where)
        return links.push(mine, mine, here.ys[sign], theirs)

    def side(y_off, where):
        waits = []
        for j in range(1, Z_LO):
            mine = chunk(buf, here.row_at(y_off, 0), where)
            theirs = chunk(buf, here.row_at(y_off, -j), where)
            waits.append(links.push(mine, mine, here.zls[j], theirs))
        return waits

    pending, last = {}, []

    def launch(tag):
        for sign in (1, -1):
            pending[tag, sign] = ring(tag, sign, 1)

    def step(tag, hop):
        for sign in (1, -1):
            pending[tag, sign]()
            if hop < far:
                pending[tag, sign] = ring(tag, sign, hop + 1)
            if tag == "B":
                last.extend(side(-sign * hop, span(tag, sign, hop)))

    launch("B")
    launch(0)
    first = side(0, span(0, 1, 1))
    last.extend(side(0, span("B", 1, 1)))
    step("B", 1)
    step(0, 1)
    for j in range(1, Z_LO):
        first[j - 1]()
        launch(j)
    for hop in range(2, far + 1):
        step("B", hop)
        step(0, hop)
        for j in range(1, Z_LO):
            step(j, hop - 1)
    for j in range(1, Z_LO):
        step(j, far)
    for wait in last:
        wait()


def tile_products(tiles, source, into, origin, total, transposed):
    slots = tiles.shape[0]
    total[slots] = jnp.zeros(total.shape[1:], F32)

    def slot(k, _):
        before = jnp.int32(slots)
        for j in range(slots):
            before = jnp.where((j < k) & (into[j] == into[k]), j, before)
        block = source[origin[k]]
        total[k] = total[before] + lax.dot_general(
            tiles[k],
            block.reshape(block.shape[0] * block.shape[1], block.shape[2]),
            (((0 if transposed else 1,), (0,)), ((), ())),
            preferred_element_type=F32,
        )
        return 0

    lax.fori_loop(0, slots, slot, 0)


def target_sum(total, into, live, target):
    slots = total.shape[0] - 1
    count = live[0]
    last = jnp.int32(slots)
    for j in range(slots):
        last = jnp.where((j < count) & (into[j] == target), j, last)
    return total[last]


ORDER = (2, 1, -1, 0)


def sum_col(here, links, tile, part, from_core, sums, x_far, x_near, z_sums, z_far, z_near):
    rows, width = part.shape[2:]
    half, quarter = rows // 2, rows // 4
    halves = (pl.ds(0, half), pl.ds(half, half))
    core = here.core
    arrived = {}

    def convert(g):
        for i, x_off in enumerate(ORDER):
            chip = here.chip_at(x_off, ORDER[g])
            part[chip] = tile(chip).astype(BF16).reshape(2, rows, width)
            slot = from_core.at[g, i]
            arrived[g, i] = links.push(part.at[chip, 1 - core], slot, here.sibling, slot)

    def pair_sum(g, i):
        if (g, i) in arrived:
            arrived.pop((g, i))()
            sums[g, i] = part[here.chip_at(ORDER[i], ORDER[g]), core] + from_core[g, i]

    def quarter_of(h, s):
        return pl.ds(h * half + (0 if s > 0 else quarter), quarter)

    waits = {}

    def x_first(b):
        g, h = b
        pair_sum(g, 0)
        for n, s in enumerate((1, -1)):
            slot = x_far.at[g, h, n]
            waits[b, "far", s] = links.push(sums.at[g, 0, quarter_of(h, s)], slot, here.xs[s], slot)

    def x_second(b):
        g, h = b
        for n, s in enumerate((1, -1)):
            pair_sum(g, 1 + n)
            waits[b, "far", s]()
            where = quarter_of(h, s)
            sums[g, 1 + n, where] = sums[g, 1 + n, where] + x_far[g, h, n]
            slot = x_near.at[g, h, n]
            waits[b, "near", s] = links.push(sums.at[g, 1 + n, halves[h]], slot, here.xs[s], slot)

    def x_last(b):
        g, h = b
        pair_sum(g, 3)
        for s in (1, -1):
            waits[b, "near", s]()
        total = sums[g, 3, halves[h]].astype(F32) + x_near[g, h, 0].astype(F32) + x_near[g, h, 1].astype(F32)
        z_sums[g, halves[h]] = total.astype(BF16)
        if g == 0:
            n, s = h, (1, -1)[h]
            slot = z_far.at[n]
            waits["z_far", s] = links.push(z_sums.at[g, halves[h]], slot, here.zhs[s], slot)
        elif g < 3:
            n, s = g - 1, ORDER[g]
            if h == n:
                waits["z_far", s]()
                z_sums[g, halves[h]] = z_sums[g, halves[h]] + z_far[n]
            slot = z_near.at[n, halves[h]]
            waits["z_near", s, h] = links.push(z_sums.at[g, halves[h]], slot, here.zhs[s], slot)

    blocks = [(0, 0), (0, 1), (1, 1), (2, 0), (1, 0), (2, 1), (3, 0), (3, 1)]
    convert(0)
    convert(1)
    x_first(blocks[0])
    x_first(blocks[1])
    convert(2)
    for n, b in enumerate(blocks):
        x_second(b)
        if n == 1:
            convert(3)
        if n + 2 < len(blocks):
            x_first(blocks[n + 2])
        if n >= 1:
            x_last(blocks[n - 1])
    x_last(blocks[-1])
    links.drain()
    for s, h in ((1, 1), (-1, 0), (1, 0), (-1, 1)):
        waits["z_near", s, h]()
    total = z_sums[3].astype(F32) + z_near[0].astype(F32) + z_near[1].astype(F32)
    return total.astype(BF16)


def gather_col(here, links, grads, between):
    rows = grads.shape[2]
    half = rows // 2
    piece = {1: pl.ds(0, half), -1: pl.ds(half, half)}
    last = []

    def at(x_off, z_off, k, where):
        return grads.at[here.chip_at(x_off, z_off), k, where]

    def to_core(x_off, z_off, where):
        mine = at(x_off, z_off, here.core, where)
        last.append(links.push(mine, mine, here.sibling, at(x_off, z_off, 1 - here.core, where)))

    def to_z(s, z_off, where):
        mine = at(0, z_off, here.core, where)
        return links.push(mine, mine, here.zhs[s], at(0, z_off - s, here.core, where))

    def to_x(s, x_off, z_off, where):
        mine = at(x_off, z_off, here.core, where)
        return links.push(mine, mine, here.xs[s], at(x_off - s, z_off, here.core, where))

    def cut(where):
        size = where.size // 2
        return {1: pl.ds(where.start, size), -1: pl.ds(where.start + size, size)}

    near, far = {}, {}

    def x_start(z_off, side):
        near[z_off, side] = {s: to_x(s, 0, z_off, piece[side]) for s in (1, -1)}
        if z_off == 2:
            near[z_off, side][2] = to_x(2, 0, z_off, piece[side])

    def x_pass(z_off, side):
        far[z_off, side] = {}
        for s in (1, -1):
            near[z_off, side][s]()
            far[z_off, side][s] = to_x(s, -s, z_off, cut(piece[side])[s])
            to_core(-s, z_off, piece[side])

    def x_end(z_off, side):
        for s in (1, -1):
            far[z_off, side][s]()
            to_core(2, z_off, cut(piece[side])[s])

    first = {s: to_z(s, 0, piece[s]) for s in (1, -1)}
    second = {s: to_z(s, 0, piece[-s]) for s in (1, -1)}
    x_start(0, 1)
    x_start(0, -1)
    to_core(0, 0, pl.ds(0, rows))
    between()
    x_pass(0, 1)
    x_pass(0, -1)
    between()
    opposite = {}
    for s in (1, -1):
        first[s]()
        opposite[s] = to_z(s, -s, piece[s])
        x_start(-s, s)
        to_core(0, -s, piece[s])
    x_end(0, 1)
    x_end(0, -1)
    for s in (1, -1):
        x_pass(-s, s)
    for s in (1, -1):
        second[s]()
        x_start(-s, -s)
        to_core(0, -s, piece[-s])
    for s in (1, -1):
        x_end(-s, s)
    between()
    for s in (1, -1):
        x_pass(-s, -s)
    for s in (1, -1):
        opposite[s]()
        x_start(2, s)
        to_core(0, 2, piece[s])
    for s in (1, -1):
        x_end(-s, -s)
    between()
    for side in (1, -1):
        for s in (1, -1):
            near[2, side][s]()
            to_core(-s, 2, piece[side])
    between()
    for side in (1, -1):
        near[2, side][2]()
        to_core(2, 2, piece[side])
    links.drain()
    for wait in last:
        wait()


def sum_row(here, links, part, a_in, a_sum, a_side, b_in, b_sum, b_side, between):
    rows = part.shape[2]
    far = here.rings // 2
    n_b = rows - SUM_PART
    part_a, part_b = pl.ds(0, SUM_PART), pl.ds(SUM_PART, n_b)
    waits = {}

    def half(count, cut, sign):
        return pl.ds(0, cut) if sign > 0 else pl.ds(cut, count - cut)

    def mine(y_off, z_off, where):
        index = here.row_at(y_off, z_off)
        return part[lax.div(index, 2), lax.rem(index, 2), where]

    def ring_send(key, hop, total, partial_in, sums):
        cut = SUM_CUTS[0] if key[0] == "A" else SUM_CUTS[1]
        count = partial_in.shape[2]
        for n, s in enumerate((1, -1)):
            at, slot = sums.at[n, hop - 1], partial_in.at[n, hop - 1]
            if hop == far:
                sums[n, hop - 1] = total(s)
                where = half(count, cut, s)
                at, slot = at.at[where], slot.at[where]
            elif hop + 1 == far:
                sums[n, hop - 1] = total(s)
                where = half(count, cut, s)
                waits[key, s]()
                sums[n, hop - 1, where] = sums[n, hop - 1, where] + partial_in[n, hop, where]
            else:
                own = total(s)
                waits[key, s]()
                sums[n, hop - 1] = own + partial_in[n, hop]
            waits[key, s] = links.push(at, slot, here.ys[s], slot)

    def ring_end(key, own, partial_in):
        for s in (1, -1):
            waits[key, s]()
        return own.astype(F32) + partial_in[0, 0].astype(F32) + partial_in[1, 0].astype(F32)

    def a_send(j, hop):
        ring_send(("A", j), hop, lambda s: mine(s * hop, j, part_a), a_in.at[j], a_sum.at[j])

    side_waits = []

    def a_across(j):
        a_side[0, j - 1] = ring_end(("A", j), mine(0, j, part_a), a_in.at[j]).astype(BF16)
        slot = a_side.at[1, j - 1]
        side_waits.append(links.push(a_side.at[0, j - 1], slot, here.zls[j], slot))

    offsets = [far] + [s * h for h in range(far - 1, 0, -1) for s in (1, -1)] + [0]
    b_waits = {}

    def b_across():
        for i, y_off in enumerate(offsets):
            b_waits[y_off] = []
            for j in range(1, Z_LO):
                slot = b_side.at[i, j - 1]
                source = chunk(part, here.row_at(y_off, j), part_b)
                b_waits[y_off].append(links.push(source, slot, here.zls[j], slot))

    def b_total(y_off):
        i = offsets.index(y_off)
        for wait in b_waits[y_off]:
            wait()
        b_waits[y_off] = []
        return mine(y_off, 0, part_b).astype(F32) + b_side[i, 0].astype(F32) + b_side[i, 1].astype(F32)

    def b_send(hop):
        ring_send(
            ("B", 0), hop, lambda s: b_total(far if hop == far else s * hop).astype(BF16), b_in, b_sum
        )

    a_send(1, far)
    a_send(2, far)
    b_across()
    a_send(0, far)
    for hop in range(far - 1, 0, -1):
        a_send(1, hop)
        a_send(2, hop)
        if hop + 2 <= far:
            b_send(hop + 2)
        if hop + 1 < far:
            a_send(0, hop + 1)
        between()
    a_across(1)
    a_across(2)
    b_send(2)
    a_send(0, 1)
    between()
    b_send(1)
    total_a = ring_end(("A", 0), mine(0, 0, part_a), a_in.at[0])
    total_b = ring_end(("B", 0), b_total(0), b_in)
    for j, wait in enumerate(side_waits):
        wait()
        total_a += a_side[1, j].astype(F32)
    return total_a.astype(BF16), total_b.astype(BF16)


def weight_sum(here, links, scale, w_half, w_out, w_core, w_y_out, w_y, w_x_out, w_x, w_lo, w_hi, w_all):
    core, y, x = here.core, here.y, here.x
    fine = w_x.shape[1]

    def pair():
        w_out[...] = w_half[1 - core].astype(BF16)
        return [links.push(w_out, w_core, here.sibling, w_core)]

    def over_y():
        w_half[core] = w_half[core] + w_core[...].astype(F32)
        w_y_out[...] = w_half[core].astype(BF16)
        return [
            links.push(w_y_out.at[wrap(y + j, here.rings)], w_y.at[j - 1], here.ys[j], w_y.at[j - 1])
            for j in range(1, here.rings)
        ]

    def over_x():
        total = w_half[core, y]
        for j in range(1, here.rings):
            total += w_y[j - 1].astype(F32)
        w_half[core, y] = total
        for i in range(here.n_x):
            w_x_out[i] = total[i * fine : (i + 1) * fine].astype(BF16)
        return [
            links.push(w_x_out.at[wrap(x + j, here.n_x)], w_x.at[j - 1], here.xs[j], w_x.at[j - 1])
            for j in range(1, here.n_x)
        ]

    def over_lo():
        total = w_half[core, y, pl.ds(x * fine, fine)]
        for j in range(1, here.n_x):
            total += w_x[j - 1].astype(F32)
        w_lo[here.zl] = total
        slot = w_lo.at[here.zl]
        return [links.push(slot, slot, here.zls[j], w_lo.at[wrap(here.zl - j, Z_LO)]) for j in range(1, Z_LO)]

    def over_hi():
        w_hi[here.zh] = w_lo[0] + w_lo[1] + w_lo[2]
        slot = w_hi.at[here.zh]
        return [links.push(slot, slot, here.zhs[j], w_hi.at[wrap(here.zh - j, Z_HI)]) for j in range(1, Z_HI)]

    def back_y():
        total = (w_hi[0] + w_hi[1]) + (w_hi[2] + w_hi[3])
        w_all[core, x, y] = (total * scale).astype(BF16)
        slot = w_all.at[core, x, y]
        return [
            links.push(slot, slot, here.ys[j], w_all.at[core, x, wrap(y - j, here.rings)])
            for j in range(1, here.rings)
        ]

    def back_x():
        slot = w_all.at[core, x]
        return [
            links.push(slot, slot, here.xs[j], w_all.at[core, wrap(x - j, here.n_x)])
            for j in range(1, here.n_x)
        ]

    def back_pair():
        return [links.push(w_all.at[core], w_all.at[core], here.sibling, w_all.at[1 - core])]

    return [pair, over_y, over_x, over_lo, over_hi, back_y, back_x, back_pair]


def kernel(
    rings,
    n_x,
    scale,
    live,
    tile_rows,
    tile_cols,
    feat_ref,
    tiles_ref,
    weight_ref,
    cot_ref,
    own_ref,
    final_ref,
    w_all,
    weight,
    cot,
    tiles,
    feats,
    total,
    part,
    from_core,
    sums,
    x_far,
    x_near,
    z_sums,
    z_far,
    z_near,
    grads,
    back,
    a_in,
    a_sum,
    a_side,
    b_in,
    b_sum,
    b_side,
    w_half,
    w_out,
    w_core,
    w_y_out,
    w_y,
    w_x_out,
    w_x,
    w_lo,
    w_hi,
    send,
    recv,
    local,
):
    here = Place(rings, n_x)
    links = Links(send, recv)
    loads = [
        pltpu.make_async_copy(source, target, local.at[i])
        for i, (source, target) in enumerate(
            (
                (feat_ref, chunk(feats, here.row)),
                (tiles_ref, tiles),
                (weight_ref, weight),
                (cot_ref, cot),
            )
        )
    ]
    for load in loads:
        load.start()
    here.greet()
    loads[0].wait()
    gather_row(here, links, feats)
    for load in loads[1:]:
        load.wait()
    tile_products(tiles, feats, tile_rows, tile_cols, total, False)
    own_sum = sum_col(
        here,
        links,
        lambda target: target_sum(total, tile_rows, live, target),
        part,
        from_core,
        sums,
        x_far,
        x_near,
        z_sums,
        z_far,
        z_near,
    )
    pre_act = jnp.dot(own_sum, weight[...], preferred_element_type=F32)
    gate = jax.nn.sigmoid(pre_act)
    own_grad = (cot[...].astype(F32) * gate * (1.0 + pre_act * (1.0 - gate))).astype(BF16)
    grads[here.chip, here.core] = own_grad

    stages = weight_sum(
        here, links, scale, w_half, w_out, w_core, w_y_out, w_y, w_x_out, w_x, w_lo, w_hi, w_all
    )
    weight_waits = []

    def weight_step():
        for wait in weight_waits:
            wait()
        del weight_waits[:]
        if stages:
            weight_waits.extend(stages.pop(0)())

    def beside_gather():
        if len(stages) == 8:
            own_ref[...] = own_sum
            term = lax.dot_general(own_sum, own_grad, (((0,), (0,)), ((), ())), preferred_element_type=F32)
            columns = term.shape[1] // 2
            for k in range(2):
                w_half[k] = term[:, k * columns : (k + 1) * columns].reshape(w_half.shape[1:])
        weight_step()

    gather_col(here, links, grads, beside_gather)
    tile_products(tiles, grads, tile_cols, tile_rows, total, True)
    rows, width = back.shape[2:]

    def store(target, _):
        back[target] = target_sum(total, tile_cols, live, target).astype(BF16).reshape(2, rows, width)
        return 0

    lax.fori_loop(0, back.shape[0], store, 0)
    weight_step()
    parts = sum_row(here, links, back, a_in, a_sum, a_side, b_in, b_sum, b_side, weight_step)
    low = 0
    for chunk_sum in parts:
        count = chunk_sum.shape[0]
        final_ref[pl.ds(low, count)] = chunk_sum
        low += count
    while stages or weight_waits:
        weight_step()
    links.drain()


def results_kernel(own_ref, final_ref, sum_ref, weight_ref, hidden_ref, grad_feat_ref, grad_weight_ref):
    pre_act = jnp.dot(own_ref[...], weight_ref[...], preferred_element_type=F32)
    hidden_ref[...] = (pre_act * jax.nn.sigmoid(pre_act)).astype(hidden_ref.dtype)
    grad_feat_ref[...] = lax.dot_general(
        final_ref[...], weight_ref[...], (((1,), (1,)), ((), ())), preferred_element_type=F32
    ).astype(grad_feat_ref.dtype)
    columns = sum_ref.shape[-1]
    for k in range(2):
        for i in range(sum_ref.shape[1]):
            grad_weight_ref[:, i, :, k * columns : (k + 1) * columns] = sum_ref[k, i].astype(F32)


def shards(features, tile_values, tile_rows, tile_cols, tile_live, weight, cotangent):
    rows, width = features.shape
    slots, edge, _ = tile_values.shape
    n_row, n_col = lax.axis_size("row"), lax.axis_size("col")
    rings, n_x = n_row // Z_LO, n_col // (2 * Z_HI)
    far, n_b = rings // 2, rows - SUM_PART
    columns, coarse = width // 2, width // rings
    fine = coarse // n_x
    vmem = pl.BlockSpec(memory_space=pltpu.VMEM)
    smem = pl.BlockSpec(memory_space=pltpu.SMEM)
    scratch = [
        pltpu.VMEM(shape, dtype)
        for shape, dtype in (
            ((width, width), BF16),
            ((rows, width), BF16),
            ((slots, edge, edge), BF16),
            ((n_row // 2, 2, rows, width), BF16),
            ((slots + 1, edge, width), F32),
            ((n_col // 2, 2, rows, width), BF16),
            ((4, 4, rows, width), BF16),
            ((4, 4, rows, width), BF16),
            ((4, 2, 2, rows // 4, width), BF16),
            ((4, 2, 2, rows // 2, width), BF16),
            ((4, rows, width), BF16),
            ((2, rows // 2, width), BF16),
            ((2, rows, width), BF16),
            ((n_col // 2, 2, rows, width), BF16),
            ((n_row // 2, 2, rows, width), BF16),
            ((Z_LO, 2, far, SUM_PART, width), BF16),
            ((Z_LO, 2, far, SUM_PART, width), BF16),
            ((2, Z_LO - 1, SUM_PART, width), BF16),
            ((2, far, n_b, width), BF16),
            ((2, far, n_b, width), BF16),
            ((rings, Z_LO - 1, n_b, width), BF16),
            ((2, rings, coarse, columns), F32),
            ((rings, coarse, columns), BF16),
            ((rings, coarse, columns), BF16),
            ((rings, coarse, columns), BF16),
            ((rings - 1, coarse, columns), BF16),
            ((n_x, fine, columns), BF16),
            ((n_x - 1, fine, columns), BF16),
            ((Z_LO, fine, columns), F32),
            ((Z_HI, fine, columns), F32),
        )
    ]
    own_sum, gathered_back, weight_total = pl.pallas_call(
        functools.partial(kernel, rings, n_x, float(rows * n_row * n_col) ** -0.5),
        out_shape=(
            jax.ShapeDtypeStruct((rows, width), BF16),
            jax.ShapeDtypeStruct((rows, width), BF16),
            jax.ShapeDtypeStruct((2, n_x, rings, fine, columns), BF16),
        ),
        in_specs=[smem] * 3 + [pl.BlockSpec(memory_space=pltpu.HBM)] * 4,
        out_specs=(vmem, vmem, vmem),
        scratch_shapes=scratch
        + [
            pltpu.SemaphoreType.DMA((320,)),
            pltpu.SemaphoreType.DMA((320,)),
            pltpu.SemaphoreType.DMA((4,)),
        ],
        compiler_params=pltpu.CompilerParams(
            collective_id=0, has_side_effects=True, vmem_limit_bytes=VMEM_LIMIT
        ),
        name="graph_layer",
    )(tile_live, tile_rows, tile_cols, features, tile_values, weight, cotangent)
    hidden, grad_features, grad_weight = pl.pallas_call(
        results_kernel,
        out_shape=(
            jax.ShapeDtypeStruct((rows, width), BF16),
            jax.ShapeDtypeStruct((rows, width), BF16),
            jax.ShapeDtypeStruct((rings, n_x, fine, width), F32),
        ),
        in_specs=[vmem] * 4,
        out_specs=(vmem, vmem, vmem),
        compiler_params=pltpu.CompilerParams(vmem_limit_bytes=VMEM_LIMIT),
        name="results",
    )(own_sum, gathered_back, weight_total, weight)
    return hidden, grad_features, grad_weight.reshape(width, width)


def solution(mesh):
    return jax.shard_map(
        shards,
        mesh=mesh,
        in_specs=(
            P(("col", "row"), None),
            P(("row", "col"), None, None),
            P(("row", "col")),
            P(("row", "col")),
            P(("row", "col")),
            P(),
            P(("row", "col"), None),
        ),
        out_specs=(P(("row", "col"), None), P(("col", "row"), None), P()),
        check_vma=False,
    )
```

```python
import functools

import jax
import jax.numpy as jnp
from jax import lax
from jax.experimental import pallas as pl
from jax.experimental.pallas import tpu as pltpu
from jax.sharding import PartitionSpec as P

MESH = pl.DeviceIdType.MESH
F32 = jnp.float32
BF16 = jnp.bfloat16
Z_LO = 3
Z_HI = 4
VMEM_LIMIT = 56 * 1024 * 1024
GATHER_PART, GATHER_CUTS = 64, (32, 32)
SUM_PART, SUM_CUTS = 80, (48, 16)


def wrap(value, size):
    return lax.rem(value + 2 * size, size)


class Links:
    def __init__(self, send, recv):
        self.send, self.recv, self.count, self.sent = send, recv, 0, []

    def push(self, src, dst, peer, lands):
        i = self.count
        self.count += 1

        def copy(source, target):
            return pltpu.make_async_remote_copy(
                src_ref=source,
                dst_ref=target,
                send_sem=self.send.at[i],
                recv_sem=self.recv.at[i],
                device_id=peer,
                device_id_type=MESH,
            )

        out = copy(src, dst)
        out.start()
        self.sent.append(out)
        return copy(lands, lands).wait_recv

    def drain(self):
        for copy in self.sent:
            copy.wait_send()
        self.sent = []


class Place:
    def __init__(self, rings, n_x):
        self.rings, self.n_x = rings, n_x
        self.row, self.col = lax.axis_index("row"), lax.axis_index("col")
        self.y, self.zl = lax.div(self.row, Z_LO), lax.rem(self.row, Z_LO)
        self.chip, self.core = lax.div(self.col, 2), lax.rem(self.col, 2)
        self.x, self.zh = lax.div(self.chip, Z_HI), lax.rem(self.chip, Z_HI)
        self.sibling = {"col": self.chip * 2 + 1 - self.core}
        self.xs = {j: {"col": self.chip_at(j, 0) * 2 + self.core} for j in range(1, n_x)}
        self.zhs = {j: {"col": self.chip_at(0, j) * 2 + self.core} for j in range(1, Z_HI)}
        self.ys = {j: {"row": self.row_at(j, 0)} for j in range(1, rings)}
        self.zls = {j: {"row": self.row_at(0, j)} for j in range(1, Z_LO)}
        for peers, size in ((self.xs, n_x), (self.zhs, Z_HI), (self.ys, rings), (self.zls, Z_LO)):
            peers[-1] = peers[size - 1]

    def chip_at(self, x_off, z_off):
        return wrap(self.x + x_off, self.n_x) * Z_HI + wrap(self.zh + z_off, Z_HI)

    def row_at(self, y_off, z_off):
        return wrap(self.y + y_off, self.rings) * Z_LO + wrap(self.zl + z_off, Z_LO)

    def greet(self):
        barrier = pltpu.get_barrier_semaphore()
        peers = [self.sibling]
        for group in (self.xs, self.zhs, self.ys, self.zls):
            peers += [peer for j, peer in group.items() if j > 0]
        for peer in peers:
            pl.semaphore_signal(barrier, inc=1, device_id=peer, device_id_type=MESH)
        pl.semaphore_wait(barrier, len(peers))


def chunk(ref, index, rows=None):
    at = ref.at[lax.div(index, 2), lax.rem(index, 2)]
    return at if rows is None else at.at[rows]


def gather_row(here, links, buf):
    rows = buf.shape[2]
    far = here.rings // 2
    parts = {"B": (GATHER_PART, rows - GATHER_PART, GATHER_CUTS[1])}
    for j in range(Z_LO):
        parts[j] = (0, GATHER_PART, GATHER_CUTS[0])

    def span(tag, sign, hop):
        low, count, cut = parts[tag]
        if hop < far:
            return pl.ds(low, count)
        return pl.ds(low, cut) if sign > 0 else pl.ds(low + cut, count - cut)

    def ring(tag, sign, hop):
        where = span(tag, sign, hop)
        z_off = 0 if tag == "B" else -tag
        mine = chunk(buf, here.row_at(-sign * (hop - 1), z_off), where)
        theirs = chunk(buf, here.row_at(-sign * hop, z_off), where)
        return links.push(mine, mine, here.ys[sign], theirs)

    def side(y_off, where):
        waits = []
        for j in range(1, Z_LO):
            mine = chunk(buf, here.row_at(y_off, 0), where)
            theirs = chunk(buf, here.row_at(y_off, -j), where)
            waits.append(links.push(mine, mine, here.zls[j], theirs))
        return waits

    pending, last = {}, []

    def launch(tag):
        for sign in (1, -1):
            pending[tag, sign] = ring(tag, sign, 1)

    def step(tag, hop):
        for sign in (1, -1):
            pending[tag, sign]()
            if hop < far:
                pending[tag, sign] = ring(tag, sign, hop + 1)
            if tag == "B":
                last.extend(side(-sign * hop, span(tag, sign, hop)))

    launch("B")
    launch(0)
    first = side(0, span(0, 1, 1))
    last.extend(side(0, span("B", 1, 1)))
    step("B", 1)
    step(0, 1)
    for j in range(1, Z_LO):
        first[j - 1]()
        launch(j)
    for hop in range(2, far + 1):
        step("B", hop)
        step(0, hop)
        for j in range(1, Z_LO):
            step(j, hop - 1)
    for j in range(1, Z_LO):
        step(j, far)
    for wait in last:
        wait()


def tile_products(tiles, source, into, origin, total, transposed):
    slots = tiles.shape[0]
    total[slots] = jnp.zeros(total.shape[1:], F32)

    def slot(k, _):
        before = jnp.int32(slots)
        for j in range(slots):
            before = jnp.where((j < k) & (into[j] == into[k]), j, before)
        block = source[origin[k]]
        total[k] = total[before] + lax.dot_general(
            tiles[k],
            block.reshape(block.shape[0] * block.shape[1], block.shape[2]),
            (((0 if transposed else 1,), (0,)), ((), ())),
            preferred_element_type=F32,
        )
        return 0

    lax.fori_loop(0, slots, slot, 0, unroll=True)


def target_sum(total, into, live, target):
    slots = total.shape[0] - 1
    count = live[0]
    last = jnp.int32(slots)
    for j in range(slots):
        last = jnp.where((j < count) & (into[j] == target), j, last)
    return total[last]


ORDER = (2, 1, -1, 0)


def sum_col(here, links, tile, part, from_core, sums, x_far, x_near, z_sums, z_far, z_near):
    rows, width = part.shape[2:]
    half, quarter = rows // 2, rows // 4
    halves = (pl.ds(0, half), pl.ds(half, half))
    core = here.core
    arrived = {}

    def convert(g):
        for i, x_off in enumerate(ORDER):
            chip = here.chip_at(x_off, ORDER[g])
            part[chip] = tile(chip).astype(BF16).reshape(2, rows, width)
            slot = from_core.at[g, i]
            arrived[g, i] = links.push(part.at[chip, 1 - core], slot, here.sibling, slot)

    def pair_sum(g, i):
        if (g, i) in arrived:
            arrived.pop((g, i))()
            sums[g, i] = part[here.chip_at(ORDER[i], ORDER[g]), core] + from_core[g, i]

    def quarter_of(h, s):
        return pl.ds(h * half + (0 if s > 0 else quarter), quarter)

    waits = {}

    def x_first(b):
        g, h = b
        pair_sum(g, 0)
        for n, s in enumerate((1, -1)):
            slot = x_far.at[g, h, n]
            waits[b, "far", s] = links.push(sums.at[g, 0, quarter_of(h, s)], slot, here.xs[s], slot)

    def x_second(b):
        g, h = b
        for n, s in enumerate((1, -1)):
            pair_sum(g, 1 + n)
            waits[b, "far", s]()
            where = quarter_of(h, s)
            sums[g, 1 + n, where] = sums[g, 1 + n, where] + x_far[g, h, n]
            slot = x_near.at[g, h, n]
            waits[b, "near", s] = links.push(sums.at[g, 1 + n, halves[h]], slot, here.xs[s], slot)

    def x_last(b):
        g, h = b
        pair_sum(g, 3)
        for s in (1, -1):
            waits[b, "near", s]()
        total = sums[g, 3, halves[h]].astype(F32) + x_near[g, h, 0].astype(F32) + x_near[g, h, 1].astype(F32)
        z_sums[g, halves[h]] = total.astype(BF16)
        if g == 0:
            n, s = h, (1, -1)[h]
            slot = z_far.at[n]
            waits["z_far", s] = links.push(z_sums.at[g, halves[h]], slot, here.zhs[s], slot)
        elif g < 3:
            n, s = g - 1, ORDER[g]
            if h == n:
                waits["z_far", s]()
                z_sums[g, halves[h]] = z_sums[g, halves[h]] + z_far[n]
            slot = z_near.at[n, halves[h]]
            waits["z_near", s, h] = links.push(z_sums.at[g, halves[h]], slot, here.zhs[s], slot)

    blocks = [(0, 0), (0, 1), (1, 1), (2, 0), (1, 0), (2, 1), (3, 0), (3, 1)]
    convert(0)
    x_first(blocks[0])
    x_first(blocks[1])
    convert(1)
    convert(2)
    for n, b in enumerate(blocks):
        x_second(b)
        if n == 1:
            convert(3)
        if n + 2 < len(blocks):
            x_first(blocks[n + 2])
        if n >= 1:
            x_last(blocks[n - 1])
    x_last(blocks[-1])
    links.drain()
    for s, h in ((1, 1), (-1, 0), (1, 0), (-1, 1)):
        waits["z_near", s, h]()
    total = z_sums[3].astype(F32) + z_near[0].astype(F32) + z_near[1].astype(F32)
    return total.astype(BF16)


def gather_col(here, links, grads, between):
    rows = grads.shape[2]
    half = rows // 2
    piece = {1: pl.ds(0, half), -1: pl.ds(half, half)}
    last = []

    def at(x_off, z_off, k, where):
        return grads.at[here.chip_at(x_off, z_off), k, where]

    def to_core(x_off, z_off, where):
        mine = at(x_off, z_off, here.core, where)
        last.append(links.push(mine, mine, here.sibling, at(x_off, z_off, 1 - here.core, where)))

    def to_z(s, z_off, where):
        mine = at(0, z_off, here.core, where)
        return links.push(mine, mine, here.zhs[s], at(0, z_off - s, here.core, where))

    def to_x(s, x_off, z_off, where):
        mine = at(x_off, z_off, here.core, where)
        return links.push(mine, mine, here.xs[s], at(x_off - s, z_off, here.core, where))

    def cut(where):
        size = where.size // 2
        return {1: pl.ds(where.start, size), -1: pl.ds(where.start + size, size)}

    near, far = {}, {}

    def x_start(z_off, side):
        near[z_off, side] = {s: to_x(s, 0, z_off, piece[side]) for s in (1, -1)}
        if z_off == 2:
            near[z_off, side][2] = to_x(2, 0, z_off, piece[side])

    def x_pass(z_off, side):
        far[z_off, side] = {}
        for s in (1, -1):
            near[z_off, side][s]()
            far[z_off, side][s] = to_x(s, -s, z_off, cut(piece[side])[s])
            to_core(-s, z_off, piece[side])

    def x_end(z_off, side):
        for s in (1, -1):
            far[z_off, side][s]()
            to_core(2, z_off, cut(piece[side])[s])

    first = {s: to_z(s, 0, piece[s]) for s in (1, -1)}
    second = {s: to_z(s, 0, piece[-s]) for s in (1, -1)}
    x_start(0, 1)
    x_start(0, -1)
    to_core(0, 0, pl.ds(0, rows))
    between()
    x_pass(0, 1)
    x_pass(0, -1)
    between()
    opposite = {}
    for s in (1, -1):
        first[s]()
        opposite[s] = to_z(s, -s, piece[s])
        x_start(-s, s)
        to_core(0, -s, piece[s])
    x_end(0, 1)
    x_end(0, -1)
    for s in (1, -1):
        x_pass(-s, s)
    for s in (1, -1):
        second[s]()
        x_start(-s, -s)
        to_core(0, -s, piece[-s])
    for s in (1, -1):
        x_end(-s, s)
    between()
    for s in (1, -1):
        x_pass(-s, -s)
    for s in (1, -1):
        opposite[s]()
        x_start(2, s)
        to_core(0, 2, piece[s])
    for s in (1, -1):
        x_end(-s, -s)
    between()
    for side in (1, -1):
        for s in (1, -1):
            near[2, side][s]()
            to_core(-s, 2, piece[side])
    between()
    for side in (1, -1):
        near[2, side][2]()
        to_core(2, 2, piece[side])
    links.drain()
    for wait in last:
        wait()


def sum_row(here, links, part, a_in, a_sum, a_side, b_in, b_sum, b_side, between):
    rows = part.shape[2]
    far = here.rings // 2
    n_b = rows - SUM_PART
    part_a, part_b = pl.ds(0, SUM_PART), pl.ds(SUM_PART, n_b)
    waits = {}

    def half(count, cut, sign):
        return pl.ds(0, cut) if sign > 0 else pl.ds(cut, count - cut)

    def mine(y_off, z_off, where):
        index = here.row_at(y_off, z_off)
        return part[lax.div(index, 2), lax.rem(index, 2), where]

    def ring_send(key, hop, total, partial_in, sums):
        cut = SUM_CUTS[0] if key[0] == "A" else SUM_CUTS[1]
        count = partial_in.shape[2]
        for n, s in enumerate((1, -1)):
            at, slot = sums.at[n, hop - 1], partial_in.at[n, hop - 1]
            if hop == far:
                sums[n, hop - 1] = total(s)
                where = half(count, cut, s)
                at, slot = at.at[where], slot.at[where]
            elif hop + 1 == far:
                sums[n, hop - 1] = total(s)
                where = half(count, cut, s)
                waits[key, s]()
                sums[n, hop - 1, where] = sums[n, hop - 1, where] + partial_in[n, hop, where]
            else:
                own = total(s)
                waits[key, s]()
                sums[n, hop - 1] = own + partial_in[n, hop]
            waits[key, s] = links.push(at, slot, here.ys[s], slot)

    def ring_end(key, own, partial_in):
        for s in (1, -1):
            waits[key, s]()
        return own.astype(F32) + partial_in[0, 0].astype(F32) + partial_in[1, 0].astype(F32)

    def a_send(j, hop):
        ring_send(("A", j), hop, lambda s: mine(s * hop, j, part_a), a_in.at[j], a_sum.at[j])

    side_waits = []

    def a_across(j):
        a_side[0, j - 1] = ring_end(("A", j), mine(0, j, part_a), a_in.at[j]).astype(BF16)
        slot = a_side.at[1, j - 1]
        side_waits.append(links.push(a_side.at[0, j - 1], slot, here.zls[j], slot))

    offsets = [far] + [s * h for h in range(far - 1, 0, -1) for s in (1, -1)] + [0]
    b_waits = {}

    def b_across():
        for i, y_off in enumerate(offsets):
            b_waits[y_off] = []
            for j in range(1, Z_LO):
                slot = b_side.at[i, j - 1]
                source = chunk(part, here.row_at(y_off, j), part_b)
                b_waits[y_off].append(links.push(source, slot, here.zls[j], slot))

    def b_total(y_off):
        i = offsets.index(y_off)
        for wait in b_waits[y_off]:
            wait()
        b_waits[y_off] = []
        return mine(y_off, 0, part_b).astype(F32) + b_side[i, 0].astype(F32) + b_side[i, 1].astype(F32)

    def b_send(hop):
        ring_send(
            ("B", 0), hop, lambda s: b_total(far if hop == far else s * hop).astype(BF16), b_in, b_sum
        )

    a_send(1, far)
    a_send(2, far)
    b_across()
    a_send(0, far)
    for hop in range(far - 1, 0, -1):
        a_send(1, hop)
        a_send(2, hop)
        if hop + 2 <= far:
            b_send(hop + 2)
        if hop + 1 < far:
            a_send(0, hop + 1)
        between()
    a_across(1)
    a_across(2)
    b_send(2)
    a_send(0, 1)
    between()
    b_send(1)
    total_a = ring_end(("A", 0), mine(0, 0, part_a), a_in.at[0])
    total_b = ring_end(("B", 0), b_total(0), b_in)
    for j, wait in enumerate(side_waits):
        wait()
        total_a += a_side[1, j].astype(F32)
    return total_a.astype(BF16), total_b.astype(BF16)


def weight_sum(here, links, scale, w_half, w_out, w_core, w_y_out, w_y, w_x_out, w_x, w_lo, w_hi, w_all):
    core, y, x = here.core, here.y, here.x
    fine = w_x.shape[1]

    def pair():
        w_out[...] = w_half[1 - core].astype(BF16)
        return [links.push(w_out, w_core, here.sibling, w_core)]

    def over_y():
        w_half[core] = w_half[core] + w_core[...].astype(F32)
        w_y_out[...] = w_half[core].astype(BF16)
        return [
            links.push(w_y_out.at[wrap(y + j, here.rings)], w_y.at[j - 1], here.ys[j], w_y.at[j - 1])
            for j in range(1, here.rings)
        ]

    def over_x():
        total = w_half[core, y]
        for j in range(1, here.rings):
            total += w_y[j - 1].astype(F32)
        w_half[core, y] = total
        for i in range(here.n_x):
            w_x_out[i] = total[i * fine : (i + 1) * fine].astype(BF16)
        return [
            links.push(w_x_out.at[wrap(x + j, here.n_x)], w_x.at[j - 1], here.xs[j], w_x.at[j - 1])
            for j in range(1, here.n_x)
        ]

    def over_lo():
        total = w_half[core, y, pl.ds(x * fine, fine)]
        for j in range(1, here.n_x):
            total += w_x[j - 1].astype(F32)
        w_lo[here.zl] = total
        slot = w_lo.at[here.zl]
        return [links.push(slot, slot, here.zls[j], w_lo.at[wrap(here.zl - j, Z_LO)]) for j in range(1, Z_LO)]

    def over_hi():
        w_hi[here.zh] = w_lo[0] + w_lo[1] + w_lo[2]
        slot = w_hi.at[here.zh]
        return [links.push(slot, slot, here.zhs[j], w_hi.at[wrap(here.zh - j, Z_HI)]) for j in range(1, Z_HI)]

    def back_y():
        total = (w_hi[0] + w_hi[1]) + (w_hi[2] + w_hi[3])
        w_all[core, x, y] = (total * scale).astype(BF16)
        slot = w_all.at[core, x, y]
        return [
            links.push(slot, slot, here.ys[j], w_all.at[core, x, wrap(y - j, here.rings)])
            for j in range(1, here.rings)
        ]

    def back_x():
        slot = w_all.at[core, x]
        return [
            links.push(slot, slot, here.xs[j], w_all.at[core, wrap(x - j, here.n_x)])
            for j in range(1, here.n_x)
        ]

    def back_pair():
        return [links.push(w_all.at[core], w_all.at[core], here.sibling, w_all.at[1 - core])]

    return [pair, over_y, over_x, over_lo, over_hi, back_y, back_x, back_pair]


def kernel(
    rings,
    n_x,
    scale,
    live_ref,
    rows_ref,
    cols_ref,
    feat_ref,
    tiles_ref,
    weight_ref,
    cot_ref,
    own_out,
    final_out,
    weight_out,
    live,
    tile_rows,
    tile_cols,
    weight,
    cot,
    tiles,
    feats,
    total,
    part,
    from_core,
    sums,
    x_far,
    x_near,
    z_sums,
    z_far,
    z_near,
    grads,
    back,
    a_in,
    a_sum,
    a_side,
    b_in,
    b_sum,
    b_side,
    w_half,
    w_out,
    w_core,
    w_y_out,
    w_y,
    w_x_out,
    w_x,
    w_lo,
    w_hi,
    w_all,
    own_ref,
    final_ref,
    send,
    recv,
    local,
):
    here = Place(rings, n_x)
    links = Links(send, recv)
    loads = [
        pltpu.make_async_copy(source, target, local.at[i])
        for i, (source, target) in enumerate(
            (
                (feat_ref, chunk(feats, here.row)),
                (tiles_ref, tiles),
                (weight_ref, weight),
                (cot_ref, cot),
                (live_ref, live),
                (rows_ref, tile_rows),
                (cols_ref, tile_cols),
            )
        )
    ]
    for load in loads:
        load.start()
    here.greet()
    loads[0].wait()
    gather_row(here, links, feats)
    for load in loads[1:]:
        load.wait()
    tile_products(tiles, feats, tile_rows, tile_cols, total, False)
    own_sum = sum_col(
        here,
        links,
        lambda target: target_sum(total, tile_rows, live, target),
        part,
        from_core,
        sums,
        x_far,
        x_near,
        z_sums,
        z_far,
        z_near,
    )
    pre_act = jnp.dot(own_sum, weight[...], preferred_element_type=F32)
    gate = jax.nn.sigmoid(pre_act)
    own_grad = (cot[...].astype(F32) * gate * (1.0 + pre_act * (1.0 - gate))).astype(BF16)
    grads[here.chip, here.core] = own_grad

    stages = weight_sum(
        here, links, scale, w_half, w_out, w_core, w_y_out, w_y, w_x_out, w_x, w_lo, w_hi, w_all
    )
    weight_waits = []

    leaving = []

    def leave(source, target):
        copy = pltpu.make_async_copy(source, target, local.at[7 + len(leaving)])
        copy.start()
        leaving.append(copy)

    def weight_step():
        for wait in weight_waits:
            wait()
        del weight_waits[:]
        if stages:
            weight_waits.extend(stages.pop(0)())
        elif len(leaving) == 1:
            leave(w_all, weight_out)

    def beside_gather():
        if len(stages) == 8:
            own_ref[...] = own_sum
            leave(own_ref, own_out)
            term = lax.dot_general(own_sum, own_grad, (((0,), (0,)), ((), ())), preferred_element_type=F32)
            columns = term.shape[1] // 2
            for k in range(2):
                w_half[k] = term[:, k * columns : (k + 1) * columns].reshape(w_half.shape[1:])
        weight_step()

    gather_col(here, links, grads, beside_gather)
    tile_products(tiles, grads, tile_cols, tile_rows, total, True)
    rows, width = back.shape[2:]

    def store(target, _):
        back[target] = target_sum(total, tile_cols, live, target).astype(BF16).reshape(2, rows, width)
        return 0

    lax.fori_loop(0, back.shape[0], store, 0)
    weight_step()
    parts = sum_row(here, links, back, a_in, a_sum, a_side, b_in, b_sum, b_side, weight_step)
    low = 0
    for chunk_sum in parts:
        count = chunk_sum.shape[0]
        final_ref[pl.ds(low, count)] = chunk_sum
        low += count
    leave(final_ref, final_out)
    links.drain()
    for copy in leaving:
        copy.wait()


def results_kernel(own_ref, final_ref, sum_ref, weight_ref, hidden_ref, grad_feat_ref, grad_weight_ref):
    pre_act = jnp.dot(own_ref[...], weight_ref[...], preferred_element_type=F32)
    hidden_ref[...] = (pre_act * jax.nn.sigmoid(pre_act)).astype(hidden_ref.dtype)
    grad_feat_ref[...] = lax.dot_general(
        final_ref[...], weight_ref[...], (((1,), (1,)), ((), ())), preferred_element_type=F32
    ).astype(grad_feat_ref.dtype)
    columns = sum_ref.shape[-1]
    for k in range(2):
        for i in range(sum_ref.shape[1]):
            grad_weight_ref[:, i, :, k * columns : (k + 1) * columns] = sum_ref[k, i].astype(F32)


def shards(features, tile_values, tile_rows, tile_cols, tile_live, weight, cotangent):
    rows, width = features.shape
    slots, edge, _ = tile_values.shape
    n_row, n_col = lax.axis_size("row"), lax.axis_size("col")
    rings, n_x = n_row // Z_LO, n_col // (2 * Z_HI)
    far, n_b = rings // 2, rows - SUM_PART
    columns, coarse = width // 2, width // rings
    fine = coarse // n_x
    vmem = pl.BlockSpec(memory_space=pltpu.VMEM)
    smem = pl.BlockSpec(memory_space=pltpu.SMEM)
    hbm = pl.BlockSpec(memory_space=pltpu.HBM)
    scratch = [
        pltpu.VMEM(shape, dtype)
        for shape, dtype in (
            ((width, width), BF16),
            ((rows, width), BF16),
            ((slots, edge, edge), BF16),
            ((n_row // 2, 2, rows, width), BF16),
            ((slots + 1, edge, width), F32),
            ((n_col // 2, 2, rows, width), BF16),
            ((4, 4, rows, width), BF16),
            ((4, 4, rows, width), BF16),
            ((4, 2, 2, rows // 4, width), BF16),
            ((4, 2, 2, rows // 2, width), BF16),
            ((4, rows, width), BF16),
            ((2, rows // 2, width), BF16),
            ((2, rows, width), BF16),
            ((n_col // 2, 2, rows, width), BF16),
            ((n_row // 2, 2, rows, width), BF16),
            ((Z_LO, 2, far, SUM_PART, width), BF16),
            ((Z_LO, 2, far, SUM_PART, width), BF16),
            ((2, Z_LO - 1, SUM_PART, width), BF16),
            ((2, far, n_b, width), BF16),
            ((2, far, n_b, width), BF16),
            ((rings, Z_LO - 1, n_b, width), BF16),
            ((2, rings, coarse, columns), F32),
            ((rings, coarse, columns), BF16),
            ((rings, coarse, columns), BF16),
            ((rings, coarse, columns), BF16),
            ((rings - 1, coarse, columns), BF16),
            ((n_x, fine, columns), BF16),
            ((n_x - 1, fine, columns), BF16),
            ((Z_LO, fine, columns), F32),
            ((Z_HI, fine, columns), F32),
            ((2, n_x, rings, fine, columns), BF16),
            ((rows, width), BF16),
            ((rows, width), BF16),
        )
    ]
    own_sum, gathered_back, weight_total = pl.pallas_call(
        functools.partial(kernel, rings, n_x, float(rows * n_row * n_col) ** -0.5),
        out_shape=(
            jax.ShapeDtypeStruct((rows, width), BF16),
            jax.ShapeDtypeStruct((rows, width), BF16),
            jax.ShapeDtypeStruct((2, n_x, rings, fine, columns), BF16),
        ),
        in_specs=[hbm] * 7,
        out_specs=(hbm, hbm, hbm),
        scratch_shapes=[pltpu.SMEM((n,), jnp.int32) for n in (1, slots, slots)]
        + scratch
        + [
            pltpu.SemaphoreType.DMA((320,)),
            pltpu.SemaphoreType.DMA((320,)),
            pltpu.SemaphoreType.DMA((10,)),
        ],
        compiler_params=pltpu.CompilerParams(
            collective_id=0, has_side_effects=True, vmem_limit_bytes=VMEM_LIMIT
        ),
        name="graph_layer",
    )(tile_live, tile_rows, tile_cols, features, tile_values, weight, cotangent)
    hidden, grad_features, grad_weight = pl.pallas_call(
        results_kernel,
        out_shape=(
            jax.ShapeDtypeStruct((rows, width), BF16),
            jax.ShapeDtypeStruct((rows, width), BF16),
            jax.ShapeDtypeStruct((rings, n_x, fine, width), F32),
        ),
        in_specs=[vmem] * 4,
        out_specs=(vmem, vmem, vmem),
        compiler_params=pltpu.CompilerParams(vmem_limit_bytes=VMEM_LIMIT),
        name="results",
    )(own_sum, gathered_back, weight_total, weight)
    return hidden, grad_features, grad_weight.reshape(width, width)


def solution(mesh):
    return jax.shard_map(
        shards,
        mesh=mesh,
        in_specs=(
            P(("col", "row"), None),
            P(("row", "col"), None, None),
            P(("row", "col")),
            P(("row", "col")),
            P(("row", "col")),
            P(),
            P(("row", "col"), None),
        ),
        out_specs=(P(("row", "col"), None), P(("col", "row"), None), P()),
        check_vma=False,
    )
```
